256 devices in a mesh: section: 4 (over y), expert: 64 (over z, x, core).
Axes of the slice: x: 4, y: 4, z: 8, core: 2. Of those that a mesh axis runs over, the one named last changes fastest.
Arguments:
- tokens_fwd: bfloat16 [512, 7168], P('expert'), may hold values from -6 to 6
- tokens_rev: bfloat16 [512, 7168], P('expert'), may hold values from -6 to 6
- routes_fwd: int32 [4, 512, 2], P('section', 'expert'), may hold values from 0 to 7, all different within a row; in each aligned block of 8 rows (0 to 7, 8 to 15, ..., all dimensions but the last counted through in order) at most 2 rows name the same one
- routes_rev: int32 [4, 512, 2], P('section', 'expert'), may hold values from 0 to 7, all different within a row; in each aligned block of 8 rows (0 to 7, 8 to 15, ..., all dimensions but the last counted through in order) at most 2 rows name the same one
- weights_fwd: bfloat16 [4, 512, 2], P('section', 'expert'), may hold values from 0.19921875 to 1
- weights_rev: bfloat16 [4, 512, 2], P('section', 'expert'), may hold values from 0.19921875 to 1
- norm_gain: bfloat16 [4, 7168], P('section'), may hold values from 0.5 to 1.5
- gate_proj: bfloat16 [4, 7168, 16384], P('section', None, 'expert'), may hold values from -0.0625 to 0.0625
- up_proj: bfloat16 [4, 7168, 16384], P('section', None, 'expert'), may hold values from -0.0625 to 0.0625
- down_proj: bfloat16 [4, 16384, 7168], P('section', 'expert'), may hold values from -0.125 to 0.125
Outputs:
- stash_fwd: bfloat16 [4, 512, 7168], P('section', 'expert')
- stash_rev: bfloat16 [4, 512, 7168], P('section', 'expert')
The draws below stay inside these ranges and needn't reach their ends.
Inputs may be any that keep to these rules, and one draw needn't show every extreme that they name: `routes_fwd`: each token names 2 different experts, and among the 8 tokens of one device of expert (aligned blocks of rows) at one section every expert is named by exactly 2 tokens. `routes_rev`: each token names 2 different experts, and among the 8 tokens of one device of expert (aligned blocks of rows) at one section every expert is named by exactly 2 tokens.
All inputs are finite; a program needn't handle non-finite values.
Results may differ from the reference program's by a relative error of at most 0.02.
Values may be sent and summed in bfloat16 or wider, within the bound.
A program may use at most 64 MiB of HBM per device.

```python
import math
import jax
import jax.numpy as jnp
import numpy as np
from jax import lax

D = 7168
FF = 2048
LIVE = 8
TOPK = 2
TOK_DEV = 8
TOKENS = 512
SLOT = 2
N_SECTION = 4
N_EXPERT = 64


def steps_of(stream_key, shape, shards, smallest, high):
    loudness = 1.0
    for position, blocks in shards:
        steps = jax.random.uniform(jax.random.fold_in(jax.random.fold_in(stream_key, 6), position), (blocks,), jnp.float32, smallest / len(shards), high / len(shards))
        loudness = loudness * jnp.repeat(jnp.exp(steps), shape[position] // blocks).reshape((-1,) + (1,) * (len(shape) - 1 - position))
    return loudness


def deal_out(rng, own, number, rows, count, top, limit, skew):
    sequence = jax.random.permutation(rng, count)
    packed, common = load_shares(count, rows * top, limit, skew, True), load_shares(count, rows * top, limit, skew, False)
    places = jnp.arange(count)

    def named(sizes, turn):
        used = int((sizes > 0).sum())
        fixed = max(1, used // 4)
        shifted = fixed + (places - fixed + turn * (used - fixed)) % max(1, count - fixed)
        return jnp.zeros((count,), jnp.int32).at[sequence[jnp.where(places < fixed, places, shifted)]].set(jnp.asarray(sizes, jnp.int32))

    sizes = jnp.where(number % 4 == 0, named(packed, number // 4), named(common, number - number // 4 - 1))
    mixed = jax.random.permutation(jax.random.fold_in(own, 3), count)
    donor, receiver = mixed[0:count // 2 * 2:2], mixed[1:count // 2 * 2:2]
    room = jnp.minimum(sizes[donor] - 1, limit - sizes[receiver]) // 2
    room = jnp.where((donor == sequence[0]) | (receiver == sequence[0]) | (sizes[receiver] == 0), 0, jnp.maximum(room, 0))
    shifted = jax.random.randint(jax.random.fold_in(own, 4), (count // 2,), 0, 1 << 20) % (room + 1)
    sizes = sizes.at[donor].add(-shifted).at[receiver].add(shifted)
    labels = jnp.searchsorted(jnp.cumsum(sizes), jnp.arange(rows * top), side="right").astype(jnp.int32)
    grid = labels.reshape(top, rows).T
    grid = grid[jax.random.permutation(jax.random.fold_in(own, 1), rows)]
    turn = jax.random.randint(jax.random.fold_in(own, 2), (rows, 1), 0, top)
    return jnp.take_along_axis(grid, (jnp.arange(top)[None, :] + turn) % top, axis=1)


def load_shares(count, total, most, slope, full):
    weights = [(1 << 20) // math.isqrt(rank ** slope) + 1 for rank in range(1, count + 1)]
    largest = most if full else min(most, max(-(-total // count), total * weights[0] // sum(weights)))
    least = 1 if total - largest >= count - 1 else 0
    counts, surplus = [largest] + [least] * (count - 1), total - largest - least * (count - 1)
    while surplus > 0:
        candidates = [i for i in range(1, count) if counts[i] < largest] or [i for i in range(1, count) if counts[i] < most]
        mass, budget = sum([weights[i] for i in candidates]), surplus
        for i in candidates:
            more = min(most - counts[i], max(1, budget * weights[i] // mass), surplus)
            counts[i] = counts[i] + more
            surplus = surplus - more
    return np.array(counts)


def noise(rng, dims, spread, bound, shards=(), kind=jnp.bfloat16):
    level = steps_of(rng, dims, shards, -0.22, 0.18) if shards else 1.0
    values = jax.random.normal(rng, dims, jnp.float32) * spread * level
    return jnp.minimum(jnp.maximum(values, -bound), bound).astype(kind)


def setup_inputs(seed: int = 0) -> dict:
    seeds = jax.random.split(jax.random.key(seed), 11)
    tokens_fwd = noise(seeds[0], (TOKENS, D), 1.0, 6.0, ((0, 64),))
    tokens_rev = noise(seeds[1], (TOKENS, D), 1.0, 6.0, ((0, 64),))
    routes_fwd_keys = jax.random.split(jax.random.fold_in(seeds[2], 1), N_SECTION * TOKENS // TOK_DEV)
    routes_fwd_turns = jax.random.permutation(jax.random.fold_in(seeds[2], 3), N_SECTION * TOKENS // TOK_DEV)
    routes_fwd = jax.vmap(lambda own, number: deal_out(jax.random.fold_in(seeds[2], 2), own, number, TOK_DEV, LIVE, TOPK, SLOT, 0))(routes_fwd_keys, routes_fwd_turns).reshape((N_SECTION, TOKENS, TOPK))
    routes_rev_keys = jax.random.split(jax.random.fold_in(seeds[3], 1), N_SECTION * TOKENS // TOK_DEV)
    routes_rev_turns = jax.random.permutation(jax.random.fold_in(seeds[3], 3), N_SECTION * TOKENS // TOK_DEV)
    routes_rev = jax.vmap(lambda own, number: deal_out(jax.random.fold_in(seeds[3], 2), own, number, TOK_DEV, LIVE, TOPK, SLOT, 0))(routes_rev_keys, routes_rev_turns).reshape((N_SECTION, TOKENS, TOPK))
    weights_fwd = jnp.clip(0.19921875 + 0.80078125 * jax.random.uniform(seeds[4], (N_SECTION, TOKENS, TOPK), jnp.float32) ** steps_of(seeds[4], (N_SECTION, TOKENS, TOPK), ((0, 4), (1, 64)), -0.2, 0.2), 0.19921875, 1.0).astype(jnp.bfloat16)
    weights_rev = jnp.clip(0.19921875 + 0.80078125 * jax.random.uniform(seeds[5], (N_SECTION, TOKENS, TOPK), jnp.float32) ** steps_of(seeds[5], (N_SECTION, TOKENS, TOPK), ((0, 4), (1, 64)), -0.2, 0.2), 0.19921875, 1.0).astype(jnp.bfloat16)
    norm_gain = jnp.clip(1.0 + 0.1 * jax.random.normal(seeds[6], (N_SECTION, D), jnp.float32), 0.5, 1.5).astype(jnp.bfloat16)
    gate_proj = noise(seeds[7], (N_SECTION, D, LIVE * FF), D ** -0.5, 0.0625, ((0, 4), (2, 64)))
    up_proj = noise(seeds[8], (N_SECTION, D, LIVE * FF), D ** -0.5, 0.0625, ((0, 4), (2, 64)))
    down_proj = noise(seeds[9], (N_SECTION, LIVE * FF, D), FF ** -0.5, 0.125, ((0, 4), (1, 64)))
    return {"tokens_fwd": tokens_fwd, "tokens_rev": tokens_rev, "routes_fwd": routes_fwd, "routes_rev": routes_rev, "weights_fwd": weights_fwd, "weights_rev": weights_rev, "norm_gain": norm_gain, "gate_proj": gate_proj, "up_proj": up_proj, "down_proj": down_proj}


def add_piece(total, pair):
    act_piece, down_piece = pair
    part = jnp.dot(act_piece, down_piece, preferred_element_type=jnp.float32).astype(jnp.bfloat16)
    part = lax.optimization_barrier(part)
    return (total + part.astype(jnp.float32), None)

def apply_layer(tokens, gain_row, gate_w, up_w, down_w, routes, weights):
    floats = tokens.astype(jnp.float32)
    scale = lax.rsqrt(lax.optimization_barrier(jnp.mean(floats * floats, axis=-1, keepdims=True)) + 1e-06)
    normed = (floats * scale * gain_row.astype(jnp.float32)).astype(jnp.bfloat16)
    experts = jnp.arange(LIVE, dtype=jnp.int32)
    table = lax.optimization_barrier(jnp.sum(weights.astype(jnp.float32)[:, :, None] * (routes[:, :, None] == experts[None, None, :]).astype(jnp.float32), axis=1))
    gate = jnp.dot(normed, gate_w, preferred_element_type=jnp.float32)
    up_val = jnp.dot(normed, up_w, preferred_element_type=jnp.float32)
    column_scale = jnp.repeat(table, FF, axis=1)
    act = (jax.nn.silu(gate) * up_val * column_scale).astype(jnp.bfloat16)
    row_count = act.shape[0]
    piece_width = act.shape[1] // N_EXPERT
    act_pieces = jnp.moveaxis(act.reshape(row_count, N_EXPERT, piece_width), 1, 0)
    down_pieces = down_w.reshape(N_EXPERT, piece_width, down_w.shape[1])
    branch, _ = lax.scan(add_piece, jnp.zeros(floats.shape, jnp.float32), (act_pieces, down_pieces))
    return (floats + branch).astype(jnp.bfloat16)

def reference(tokens_fwd, tokens_rev, routes_fwd, routes_rev, weights_fwd, weights_rev, norm_gain, gate_proj, up_proj, down_proj):
    forward_list = []
    current = tokens_fwd
    for section_num in range(N_SECTION):
        current = apply_layer(current, norm_gain[section_num], gate_proj[section_num], up_proj[section_num], down_proj[section_num], routes_fwd[section_num], weights_fwd[section_num])
        forward_list.append(current)
    reverse_list = [None] * N_SECTION
    current = tokens_rev
    for section_num in reversed(range(N_SECTION)):
        current = apply_layer(current, norm_gain[section_num], gate_proj[section_num], up_proj[section_num], down_proj[section_num], routes_rev[section_num], weights_rev[section_num])
        reverse_list[section_num] = current
    return (jnp.stack(forward_list), jnp.stack(reverse_list))
```

```python
import functools

import jax
import jax.numpy as jnp
from jax import lax
from jax.experimental import pallas as pl
from jax.experimental.pallas import tpu as pltpu
from jax.sharding import PartitionSpec as P

MESH = pl.DeviceIdType.MESH
NS, NZ, NX, NC = 4, 8, 4, 2
NP = NX * NC
TOK = 8
SLOT = 2
D = 7168
PIECE = 256
FS = D // NP
HALF = D // NC
ROWS = NZ * NP * SLOT
BLK = NP * SLOT
PT = NP * TOK
BF, F32 = jnp.bfloat16, jnp.float32


def far_first(i):
    return 4 + (1 - 2 * (i % 2)) * ((i + 1) // 2)


def nt_dot(a, b):
    return lax.dot_general(a, b, (((1,), (1,)), ((), ())), preferred_element_type=F32)


def kernel(
    tokf_ref, tokr_ref, rf_ref, rr_ref, wf_ref, wr_ref, gain_ref, gate_hbm, up_hbm, down_hbm,
    outf_ref, outr_ref,
    wg, wu, wd, tall, tokx, xin, sown, snext, wcomb, rin, acc, ssq, guout, guin, act,
    pout, pown, pin, ret, retin, dout, dinit, xres, xnew, st_out, st_in,
    t_ss, t_rs, tok_ss, tok_rs, s_ss, s_rs, wl_s, w_ss, w_rs,
    d_ss, d_rs, di_ss, ag_ss, ag_rs, gu_ss, gu_rs, p_ss, p_rs, r_ss, r_rs, x_ss, x_rs, st_ss, st_rs,
):
    s = lax.axis_index("section")
    i = lax.axis_index("expert")
    z, p = i // NP, i % NP
    x, c = p // NC, p % NC
    outer = (s == 0) | (s == NS - 1)
    low = s < NS // 2

    def at(sec, zz, pp):
        return (sec, zz * NP + pp)

    def plane(r):
        return at(s, z, (p + r) % NP)

    def xpeer(d):
        return at(s, z, ((x + d) % NX) * NC + c)

    def zpeer(k):
        return at(s, (z + k) % NZ, p)

    sib = at(s, z, x * NC + 1 - c)
    up_sec, down_sec = (s + 1) % NS, (s + NS - 1) % NS

    def remote(src, dst, ss, rs, dev):
        return pltpu.make_async_remote_copy(
            src_ref=src, dst_ref=dst, send_sem=ss, recv_sem=rs, device_id=dev, device_id_type=MESH
        )

    def loop(n, f):
        def step(n_, carry):
            f(n_)
            return carry

        lax.fori_loop(0, n, step, 0)

    bar = pltpu.get_barrier_semaphore()

    def greet(dev):
        pl.semaphore_signal(bar, inc=1, device_id=dev, device_id_type=MESH)

    loop(NP - 1, lambda r: greet(plane(r + 1)))
    loop(NZ - 1, lambda k: greet(zpeer(k + 1)))
    loop(NZ, lambda k: greet(at(up_sec, (z + k) % NZ, p)))
    loop(NZ, lambda k: greet(at(down_sec, (z + k) % NZ, p)))

    def local_weights():
        cps = [
            pltpu.make_async_copy(gate_hbm.at[0, pl.ds(c * HALF, HALF), :], wg.at[c], wl_s.at[0]),
            pltpu.make_async_copy(up_hbm.at[0, pl.ds(c * HALF, HALF), :], wu.at[c], wl_s.at[1]),
        ]
        for q in range(NX):
            cps.append(
                pltpu.make_async_copy(
                    down_hbm.at[0, :, pl.ds(pl.multiple_of(c * HALF + q * FS, 128), FS)],
                    wd.at[q, pl.ds(c * PIECE, PIECE), :],
                    wl_s.at[2 + q],
                )
            )
        return cps

    def sibling_weights():
        o = 1 - c
        cps = [
            remote(gate_hbm.at[0, pl.ds(o * HALF, HALF), :], wg.at[c], w_ss.at[0], w_rs.at[0], sib),
            remote(up_hbm.at[0, pl.ds(o * HALF, HALF), :], wu.at[c], w_ss.at[1], w_rs.at[1], sib),
        ]
        for q in range(NX):
            cps.append(
                remote(
                    down_hbm.at[0, :, pl.ds(pl.multiple_of(o * HALF + q * FS, 128), FS)],
                    wd.at[q, pl.ds(c * PIECE, PIECE), :],
                    w_ss.at[2 + q],
                    w_rs.at[2 + q],
                    sib,
                )
            )
        return cps

    for cp in local_weights():
        cp.start()

    lane = lax.broadcasted_iota(jnp.int32, (TOK, 128), 1)
    for b, (routes, weights) in enumerate(((rf_ref, wf_ref), (rr_ref, wr_ref))):
        r0, r1 = routes[0, :, 0:1], routes[0, :, 1:2]
        w0, w1 = weights[0, :, 0:1].astype(F32), weights[0, :, 1:2].astype(F32)
        mask = jnp.where((r0 == lane) | (r1 == lane), 1.0, 0.0)
        wt = jnp.where(r0 == lane - NZ, w0, 0.0) + jnp.where(r1 == lane - NZ, w1, 0.0)
        tall[p, b * TOK : (b + 1) * TOK, :] = mask + wt

    @pl.when(outer)
    def _():
        first = s == 0
        for q in range(NP):
            f = (q % NC) * NX + q // NC
            sl = slice(f * FS, (f + 1) * FS)
            tokx[q] = jnp.where(first, tokf_ref[:, sl].astype(F32), tokr_ref[:, sl].astype(F32))

    pl.semaphore_wait(bar, NP - 1 + NZ - 1 + 2 * NZ)

    def t_copy(r):
        return remote(tall.at[p], tall.at[p], t_ss.at[r], t_rs.at[r], plane(r + 1))

    def t_wait(r):
        q = (p + NP - r - 1) % NP
        remote(tall.at[q], tall.at[q], t_ss.at[r], t_rs.at[r], plane(r + 1)).wait_recv()

    def tok_copy(r):
        return remote(tokx.at[(p + r + 1) % NP], xin.at[p], tok_ss.at[r], tok_rs.at[r], plane(r + 1))

    def tok_wait(r):
        q = (p + NP - r - 1) % NP
        remote(tokx.at[q], xin.at[q], tok_ss.at[r], tok_rs.at[r], plane(r + 1)).wait_recv()

    loop(NP - 1, lambda r: t_copy(r).start())

    @pl.when(outer)
    def _():
        loop(NP - 1, lambda r: tok_copy(r).start())

    for cp in sibling_weights():
        cp.start()

    @pl.when(outer)
    def _():
        xin[p] = tokx[p]

    loop(NP - 1, t_wait)

    row = lax.broadcasted_iota(jnp.int32, (ROWS, 128), 0)
    col = lax.broadcasted_iota(jnp.int32, (ROWS, 128), 1)
    pick = jnp.where(col == (z + row // BLK) % NZ, 1.0, 0.0)
    pick_w = jnp.where(col - NZ == (z + row // BLK) % NZ, 1.0, 0.0)
    ti = lax.broadcasted_iota(jnp.int32, (PT, PT), 0)
    tj = lax.broadcasted_iota(jnp.int32, (PT, PT), 1)
    before = jnp.where((ti // TOK == tj // TOK) & (tj < ti), 1.0, 0.0)
    srow = lax.broadcasted_iota(jnp.int32, (ROWS, PT), 0)
    scol = lax.broadcasted_iota(jnp.int32, (ROWS, PT), 1)
    trow = lax.broadcasted_iota(jnp.int32, (PT, ROWS), 0)
    tcol = lax.broadcasted_iota(jnp.int32, (PT, ROWS), 1)
    for b in range(2):
        t = tall[:, b * TOK : (b + 1) * TOK, :].reshape(PT, 128)
        rank = jnp.dot(before, t, preferred_element_type=F32)
        here = nt_dot(pick, t) * jnp.where(srow // SLOT % NP == scol // TOK, 1.0, 0.0)
        right = jnp.where(nt_dot(pick, rank) == (srow % SLOT).astype(F32), 1.0, 0.0)
        sown[b, :, 0:PT] = (here * right).astype(BF)
        sown[b, :, PT:128] = jnp.zeros((ROWS, 128 - PT), BF)
        here = nt_dot(t, pick_w) * jnp.where(tcol // SLOT % NP == trow // TOK, 1.0, 0.0)
        right = jnp.where(nt_dot(rank, pick) == (tcol % SLOT).astype(F32), 1.0, 0.0)
        wcomb[b] = (here * right).astype(BF)

    def s_copy(b):
        sec = down_sec if b == 0 else up_sec
        return remote(sown.at[b], snext.at[b], s_ss.at[b], s_rs.at[b], at(sec, z, p))

    for b in range(2):
        s_copy(b).start()

    def di_copy(k):
        return remote(dinit.at[k], rin.at[0, 0, (NZ - k) % NZ], di_ss.at[k], d_rs.at[0, (NZ - k) % NZ], zpeer(k))

    @pl.when(outer)
    def _():
        loop(NP - 1, tok_wait)
        xb = xin[...].reshape(PT, FS).astype(BF)
        xres[0] = xb
        sel = jnp.where(s == 0, sown[0, :, 0:PT], sown[1, :, 0:PT])
        picked = jnp.dot(sel, xb, preferred_element_type=F32).astype(BF)
        dinit[...] = picked.reshape(NZ, BLK, FS)
        loop(NZ - 1, lambda n: di_copy(far_first(n)).start())
        rin[0, 0, 0] = picked[0:BLK]

    def job(j, carry):
        b = jnp.where(low, j, 1 - j)
        step = 1 - 2 * b
        initial = outer & (j == 0)
        to = s + step
        has_next = (to >= 0) & (to < NS)
        to = jnp.clip(to, 0, NS - 1)
        jn = jnp.where(to < NS // 2, b, 1 - b)
        came = jnp.where(initial, s, jnp.clip(s - step, 0, NS - 1))

        def d_wait(k):
            remote(rin.at[j, 0, k], rin.at[j, 0, k], di_ss.at[k], d_rs.at[j, k], zpeer(4)).wait_recv()

        def ag_copy(d, k):
            return remote(
                rin.at[j, 0, k], rin.at[j, d, k], ag_ss.at[j, d - 1, k], ag_rs.at[j, d - 1, k], xpeer(d)
            )

        def relay(n):
            k = (NZ - far_first(n)) % NZ

            @pl.when(jnp.logical_not(initial & (k == 0)))
            def _():
                d_wait(k)

            for d in (2, 1, 3):
                ag_copy(d, k).start()

        loop(NZ, relay)

        @pl.when(j == 0)
        def _():
            cps = local_weights()
            cps[0].wait()
            cps[1].wait()
            cps = sibling_weights()
            cps[0].wait_recv()
            cps[1].wait_recv()

        def slice_product(d, first):
            q = (x + NX - d) % NX
            rows = rin[j, d].reshape(ROWS, FS).astype(F32)
            g = gain_ref[:, pl.ds(pl.multiple_of(c * HALF + q * FS, 128), FS)].astype(F32)
            ss = jnp.sum(rows * rows, axis=1, keepdims=True)
            u = (rows * g).astype(BF)
            at_row = pl.ds(pl.multiple_of(q * FS, 128), FS)
            for n, w in enumerate((wg, wu)):
                for h in range(NC):
                    sl = slice((n * NC + h) * PIECE, (n * NC + h + 1) * PIECE)
                    part = jnp.dot(u, w[h, at_row, :], preferred_element_type=F32)
                    acc[:, sl] = part if first else acc[:, sl] + part
            ss = jnp.broadcast_to(ss, (ROWS, 128))
            ssq[...] = ss if first else ssq[...] + ss

        slice_product(0, True)
        for d in (1, 3, 2):
            loop(NZ, lambda k, d=d: ag_copy(d, k).wait_recv())
            slice_product(d, False)

        wide = 2 * NC * PIECE
        guout[j, :, 0:wide] = acc[...].astype(BF)
        ss = ssq[...]
        hi = ss.astype(BF)
        lo = (ss - hi.astype(F32)).astype(BF)
        lanes = lax.broadcasted_iota(jnp.int32, (ROWS, 128), 1)
        guout[j, :, wide:] = jnp.where(lanes == 0, hi, lo)
        gu = remote(guout.at[j], guin.at[j], gu_ss.at[j], gu_rs.at[j], sib)
        gu.start()
        gu.wait_recv()
        ss = ss[:, 0:1] + guin[j, :, wide : wide + 1].astype(F32) + guin[j, :, wide + 1 : wide + 2].astype(F32)
        scale = lax.rsqrt(ss * (1.0 / D) + 1e-06)
        hid = NC * PIECE
        gate = (acc[:, 0:hid] + guin[j, :, 0:hid].astype(F32)) * scale
        upv = (acc[:, hid:wide] + guin[j, :, hid:wide].astype(F32)) * scale
        act[...] = (gate / (1.0 + jnp.exp(-gate)) * upv).astype(BF)

        @pl.when(j == 0)
        def _():
            for cp in local_weights()[2:]:
                cp.wait()
            for cp in sibling_weights()[2:]:
                cp.wait_recv()

        def p_copy(d, k):
            return remote(
                pout.at[j, d - 1, k], pin.at[j, d - 1, k], p_ss.at[j, d - 1, k], p_rs.at[j, d - 1, k], xpeer(d)
            )

        for d in (2, 1, 3, 0):
            part = jnp.dot(act[...], wd[(x + d) % NX], preferred_element_type=F32)
            if d:
                pout[j, d - 1] = part.astype(BF).reshape(NZ, BLK, FS)
                loop(NZ, lambda n, d=d: p_copy(d, far_first(n)).start())
            else:
                pown[...] = part.reshape(NZ, BLK, FS)

        def r_copy(k):
            return remote(
                ret.at[j, k], retin.at[j, (NZ - k) % NZ], r_ss.at[j, k], r_rs.at[j, (NZ - k) % NZ], zpeer(k)
            )

        def give_back(n):
            k = far_first(n)
            for d in (1, 2, 3):
                p_copy(d, k).wait_recv()
            total = pown[k]
            for d in (1, 2, 3):
                total = total + pin[j, d - 1, k].astype(F32)
            total = total.astype(BF)

            @pl.when(k != 0)
            def _():
                ret[j, k] = total
                r_copy(k).start()

            @pl.when(k == 0)
            def _():
                retin[j, 0] = total

        loop(NZ, give_back)

        def x_copy():
            return remote(xnew.at[j], xres.at[jn], x_ss.at[j], x_rs.at[jn], at(to, z, p))

        def r_wait(n):
            k = n + 1
            remote(retin.at[j, k], retin.at[j, k], r_ss.at[j, k], r_rs.at[j, k], zpeer(k)).wait_recv()

        @pl.when(jnp.logical_not(initial))
        def _():
            remote(xres.at[j], xres.at[j], x_ss.at[j], x_rs.at[j], at(came, z, p)).wait_recv()

        @pl.when(j == 0)
        def _():
            for b_ in range(2):
                s_copy(b_).wait_recv()

        loop(NZ - 1, r_wait)
        branch = jnp.dot(wcomb[b], retin[j].reshape(ROWS, FS), preferred_element_type=F32)
        fresh = (xres[j].astype(F32) + branch).astype(BF)

        @pl.when(has_next)
        def _():
            picked = jnp.dot(snext[b, :, 0:PT], fresh, preferred_element_type=F32).astype(BF)
            dout[j] = picked.reshape(NZ, BLK, FS)

            def send(n):
                k = far_first(n)
                remote(
                    dout.at[j, k], rin.at[jn, 0, (NZ - k) % NZ], d_ss.at[j, k], d_rs.at[jn, (NZ - k) % NZ],
                    at(to, (z + k) % NZ, p),
                ).start()

            loop(NZ, send)
            xnew[j] = fresh
            x_copy().start()

        st_out[j] = fresh.astype(F32).reshape(NP, TOK, FS)
        st_in[j, p] = st_out[j, p]

        def st_copy(r):
            return remote(
                st_out.at[j, (p + r + 1) % NP], st_in.at[j, p], st_ss.at[j, r], st_rs.at[j, r], plane(r + 1)
            )

        loop(NP - 1, lambda r: st_copy(r).start())

        return carry

    lax.fori_loop(0, 2, job, 0)

    def st_wait(n):
        j, r = n // (NP - 1), n % (NP - 1)
        q = (p + NP - r - 1) % NP
        remote(st_out.at[j, q], st_in.at[j, q], st_ss.at[j, r], st_rs.at[j, r], plane(r + 1)).wait()

    loop(2 * (NP - 1), st_wait)
    jf = jnp.where(low, 0, 1)
    for q in range(NP):
        f = (q % NC) * NX + q // NC
        outf_ref[0, :, f * FS : (f + 1) * FS] = st_in[jf, q].astype(BF)
        outr_ref[0, :, f * FS : (f + 1) * FS] = st_in[1 - jf, q].astype(BF)

    loop(NP - 1, lambda r: t_copy(r).wait_send())
    for b in range(2):
        s_copy(b).wait_send()
    for cp in sibling_weights():
        cp.wait_send()

    @pl.when(outer)
    def _():
        loop(NP - 1, lambda r: tok_copy(r).wait_send())
        loop(NZ - 1, lambda k: di_copy(k + 1).wait_send())

    def drain(j):
        b = jnp.where(low, j, 1 - j)
        to = s + 1 - 2 * b

        @pl.when((to >= 0) & (to < NS))
        def _():
            loop(NZ, lambda k: remote(dout.at[j, k], dout.at[j, k], d_ss.at[j, k], d_rs.at[j, k], zpeer(4)).wait_send())
            remote(xnew.at[j], xnew.at[j], x_ss.at[j], x_rs.at[j], zpeer(4)).wait_send()

        def ag(k):
            for d in (1, 2, 3):
                remote(rin.at[j, 0, k], rin.at[j, d, k], ag_ss.at[j, d - 1, k], ag_rs.at[j, d - 1, k], xpeer(d)).wait_send()
                remote(
                    pout.at[j, d - 1, k], pin.at[j, d - 1, k], p_ss.at[j, d - 1, k], p_rs.at[j, d - 1, k], xpeer(d)
                ).wait_send()

        loop(NZ, ag)
        remote(guout.at[j], guin.at[j], gu_ss.at[j], gu_rs.at[j], sib).wait_send()
        loop(
            NZ - 1,
            lambda k: remote(
                ret.at[j, k + 1], ret.at[j, k + 1], r_ss.at[j, k + 1], r_rs.at[j, k + 1], zpeer(4)
            ).wait_send(),
        )

    loop(2, drain)


def run(tokens_fwd, tokens_rev, routes_fwd, routes_rev, weights_fwd, weights_rev, norm_gain, gate_proj, up_proj, down_proj):
    vmem = pl.BlockSpec(memory_space=pltpu.VMEM)
    hbm = pl.BlockSpec(memory_space=pl.ANY)
    dma = pltpu.SemaphoreType.DMA
    out = jax.ShapeDtypeStruct((1, TOK, D), BF)
    wide = 2 * NC * PIECE
    return pl.pallas_call(
        kernel,
        name="moe_pipeline",
        out_shape=(out, out),
        in_specs=[vmem] * 7 + [hbm] * 3,
        out_specs=(vmem, vmem),
        scratch_shapes=[
            pltpu.VMEM((NC, HALF, PIECE), BF),
            pltpu.VMEM((NC, HALF, PIECE), BF),
            pltpu.VMEM((NX, NC * PIECE, FS), BF),
            pltpu.VMEM((NP, 2 * TOK, 128), F32),
            pltpu.VMEM((NP, TOK, FS), F32),
            pltpu.VMEM((NP, TOK, FS), F32),
            pltpu.VMEM((2, ROWS, 128), BF),
            pltpu.VMEM((2, ROWS, 128), BF),
            pltpu.VMEM((2, PT, ROWS), BF),
            pltpu.VMEM((2, NX, NZ, BLK, FS), BF),
            pltpu.VMEM((ROWS, wide), F32),
            pltpu.VMEM((ROWS, 128), F32),
            pltpu.VMEM((2, ROWS, wide + 128), BF),
            pltpu.VMEM((2, ROWS, wide + 128), BF),
            pltpu.VMEM((ROWS, NC * PIECE), BF),
            pltpu.VMEM((2, NX - 1, NZ, BLK, FS), BF),
            pltpu.VMEM((NZ, BLK, FS), F32),
            pltpu.VMEM((2, NX - 1, NZ, BLK, FS), BF),
            pltpu.VMEM((2, NZ, BLK, FS), BF),
            pltpu.VMEM((2, NZ, BLK, FS), BF),
            pltpu.VMEM((2, NZ, BLK, FS), BF),
            pltpu.VMEM((NZ, BLK, FS), BF),
            pltpu.VMEM((2, PT, FS), BF),
            pltpu.VMEM((2, PT, FS), BF),
            pltpu.VMEM((2, NP, TOK, FS), F32),
            pltpu.VMEM((2, NP, TOK, FS), F32),
            dma((NP - 1,)), dma((NP - 1,)), dma((NP - 1,)), dma((NP - 1,)), dma((2,)), dma((2,)),
            dma((2 + NX,)), dma((2 + NX,)), dma((2 + NX,)),
            dma((2, NZ)), dma((2, NZ)), dma((NZ,)),
            dma((2, NX - 1, NZ)), dma((2, NX - 1, NZ)), dma((2,)), dma((2,)),
            dma((2, NX - 1, NZ)), dma((2, NX - 1, NZ)), dma((2, NZ)), dma((2, NZ)),
            dma((2,)), dma((2,)), dma((2, NP - 1)), dma((2, NP - 1)),
        ],
        compiler_params=pltpu.CompilerParams(
            collective_id=0, has_side_effects=True, vmem_limit_bytes=56 * 2**20
        ),
    )(tokens_fwd, tokens_rev, routes_fwd, routes_rev, weights_fwd, weights_rev, norm_gain, gate_proj, up_proj, down_proj)


def solution(mesh):
    placed = (
        P("expert", None),
        P("expert", None),
        P("section", "expert", None),
        P("section", "expert", None),
        P("section", "expert", None),
        P("section", "expert", None),
        P("section", None),
        P("section", None, "expert"),
        P("section", None, "expert"),
        P("section", "expert", None),
    )
    return jax.shard_map(
        run,
        mesh=mesh,
        in_specs=placed,
        out_specs=(P("section", "expert", None), P("section", "expert", None)),
        check_vma=False,
    )
```

```python
import functools

import jax
import jax.numpy as jnp
from jax import lax
from jax.experimental import pallas as pl
from jax.experimental.pallas import tpu as pltpu
from jax.sharding import PartitionSpec as P

MESH = pl.DeviceIdType.MESH
NS, NZ, NX, NC = 4, 8, 4, 2
NP = NX * NC
TOK = 8
LIVE = NZ
TOPK = 2
SLOT = 2
D = 7168
PIECE = 256
FS = D // NP
HALF = D // NC
ROWS = NZ * NP * SLOT
BLK = NP * SLOT
PT = NP * TOK
NH = 2
NB = NZ // NH
HROWS = ROWS // NH
OFFSETS = ((4, 2, 6, 0), (3, 5, 1, 7))
FAR_FIRST = (4, 3, 5, 2, 6, 1, 7, 0)
GRP = 2
BF, F32 = jnp.bfloat16, jnp.float32


def place(k):
    return OFFSETS[k % NH].index(-k % NZ)


def nt_dot(a, b):
    return lax.dot_general(a, b, (((1,), (1,)), ((), ())), preferred_element_type=F32)


def kernel(
    tokf_ref, tokr_ref, rf_ref, rr_ref, wf_ref, wr_ref, gain_ref, gate_hbm, up_hbm, down_hbm,
    outf_ref, outr_ref,
    wg, wu, wd, tall, tokx, xin, sown, snext, wcomb, rin, acc, ssq, guout, guin, act,
    pout, pown, pin, ret, retin, dout, dinit, xres, xnew, st_out, st_in,
    t_ss, t_rs, tok_ss, tok_rs, s_ss, s_rs, wl_s, w_ss, w_rs,
    d_ss, d_rs, di_ss, ag_ss, ag_rs, gu_ss, gu_rs, p_ss, p_rs, r_ss, r_rs, x_ss, x_rs, st_ss, st_rs,
):
    s = lax.axis_index("section")
    i = lax.axis_index("expert")
    z, p = i // NP, i % NP
    x, c = p // NC, p % NC
    outer = (s == 0) | (s == NS - 1)
    low = s < NS // 2

    def at(sec, zz, pp):
        return (sec, zz * NP + pp)

    def plane(r):
        return at(s, z, (p + r) % NP)

    def xpeer(d):
        return at(s, z, ((x + d) % NX) * NC + c)

    def zpeer(k):
        return at(s, (z + k) % NZ, p)

    sib = at(s, z, x * NC + 1 - c)
    up_sec, down_sec = (s + 1) % NS, (s + NS - 1) % NS

    def remote(src, dst, ss, rs, dev):
        return pltpu.make_async_remote_copy(
            src_ref=src, dst_ref=dst, send_sem=ss, recv_sem=rs, device_id=dev, device_id_type=MESH
        )

    def loop(n, f):
        def step(n_, carry):
            f(n_)
            return carry

        lax.fori_loop(0, n, step, 0)

    bar = pltpu.get_barrier_semaphore()

    def greet(dev):
        pl.semaphore_signal(bar, inc=1, device_id=dev, device_id_type=MESH)

    loop(NP - 1, lambda r: greet(plane(r + 1)))
    loop(NZ - 1, lambda k: greet(zpeer(k + 1)))
    loop(NZ, lambda k: greet(at(up_sec, (z + k) % NZ, p)))
    loop(NZ, lambda k: greet(at(down_sec, (z + k) % NZ, p)))

    def local_weights():
        cps = [
            pltpu.make_async_copy(gate_hbm.at[0, pl.ds(c * HALF, HALF), :], wg.at[c], wl_s.at[0]),
            pltpu.make_async_copy(up_hbm.at[0, pl.ds(c * HALF, HALF), :], wu.at[c], wl_s.at[1]),
        ]
        for q in range(NX):
            cps.append(
                pltpu.make_async_copy(
                    down_hbm.at[0, :, pl.ds(pl.multiple_of(c * HALF + q * FS, 128), FS)],
                    wd.at[q, pl.ds(c * PIECE, PIECE), :],
                    wl_s.at[2 + q],
                )
            )
        return cps

    def sibling_weights():
        o = 1 - c
        cps = [
            remote(gate_hbm.at[0, pl.ds(o * HALF, HALF), :], wg.at[c], w_ss.at[0], w_rs.at[0], sib),
            remote(up_hbm.at[0, pl.ds(o * HALF, HALF), :], wu.at[c], w_ss.at[1], w_rs.at[1], sib),
        ]
        for q in range(NX):
            cps.append(
                remote(
                    down_hbm.at[0, :, pl.ds(pl.multiple_of(o * HALF + q * FS, 128), FS)],
                    wd.at[q, pl.ds(c * PIECE, PIECE), :],
                    w_ss.at[2 + q],
                    w_rs.at[2 + q],
                    sib,
                )
            )
        return cps

    for cp in local_weights():
        cp.start()

    ei = lax.broadcasted_iota(jnp.int32, (2 * LIVE, TOK), 0)
    eye = jnp.where(
        lax.broadcasted_iota(jnp.int32, (TOK, TOK), 0) == lax.broadcasted_iota(jnp.int32, (TOK, TOK), 1), 1.0, 0.0
    )
    for b, (routes, weights) in enumerate(((rf_ref, wf_ref), (rr_ref, wr_ref))):
        turned = jnp.zeros((2 * LIVE, TOK), F32)
        for n in range(TOPK):
            route, weight = routes[n : n + 1, :], weights[n : n + 1, :].astype(F32)
            turned += jnp.where(route == ei, 1.0, 0.0) + jnp.where(route == ei - LIVE, weight, 0.0)
        tall[p, b * TOK : (b + 1) * TOK, :] = jnp.zeros((TOK, 128), F32)
        tall[p, b * TOK : (b + 1) * TOK, 0 : 2 * LIVE] = nt_dot(eye, turned)

    @pl.when(outer)
    def _():
        first = s == 0
        for q in range(NP):
            f = (q % NC) * NX + q // NC
            sl = slice(f * FS, (f + 1) * FS)
            tokx[q] = jnp.where(first, tokf_ref[:, sl].astype(F32), tokr_ref[:, sl].astype(F32))

    pl.semaphore_wait(bar, NP - 1 + NZ - 1 + 2 * NZ)

    def t_copy(r):
        return remote(tall.at[p], tall.at[p], t_ss.at[r], t_rs.at[r], plane(r + 1))

    def t_wait(r):
        q = (p + NP - r - 1) % NP
        remote(tall.at[q], tall.at[q], t_ss.at[r], t_rs.at[r], plane(r + 1)).wait_recv()

    def tok_copy(r):
        return remote(tokx.at[(p + r + 1) % NP], xin.at[p], tok_ss.at[r], tok_rs.at[r], plane(r + 1))

    def tok_wait(r):
        q = (p + NP - r - 1) % NP
        remote(tokx.at[q], xin.at[q], tok_ss.at[r], tok_rs.at[r], plane(r + 1)).wait_recv()

    loop(NP - 1, lambda r: t_copy(r).start())

    @pl.when(outer)
    def _():
        loop(NP - 1, lambda r: tok_copy(r).start())

    for cp in sibling_weights():
        cp.start()

    @pl.when(outer)
    def _():
        xin[p] = tokx[p]

    loop(NP - 1, t_wait)

    row = lax.broadcasted_iota(jnp.int32, (ROWS, 128), 0)
    col = lax.broadcasted_iota(jnp.int32, (ROWS, 128), 1)
    pick = jnp.where(col == (z + row // BLK) % NZ, 1.0, 0.0)
    pick_w = jnp.where(col - NZ == (z + row // BLK) % NZ, 1.0, 0.0)
    ti = lax.broadcasted_iota(jnp.int32, (PT, PT), 0)
    tj = lax.broadcasted_iota(jnp.int32, (PT, PT), 1)
    before = jnp.where((ti // TOK == tj // TOK) & (tj < ti), 1.0, 0.0)
    srow = lax.broadcasted_iota(jnp.int32, (ROWS, PT), 0)
    scol = lax.broadcasted_iota(jnp.int32, (ROWS, PT), 1)
    trow = lax.broadcasted_iota(jnp.int32, (PT, ROWS), 0)
    tcol = lax.broadcasted_iota(jnp.int32, (PT, ROWS), 1)
    for b in range(2):
        t = tall[:, b * TOK : (b + 1) * TOK, :].reshape(PT, 128)
        rank = jnp.dot(before, t, preferred_element_type=F32)
        here = nt_dot(pick, t) * jnp.where(srow // SLOT % NP == scol // TOK, 1.0, 0.0)
        right = jnp.where(nt_dot(pick, rank) == (srow % SLOT).astype(F32), 1.0, 0.0)
        sown[b, :, 0:PT] = (here * right).astype(BF)
        sown[b, :, PT:128] = jnp.zeros((ROWS, 128 - PT), BF)
        here = nt_dot(t, pick_w) * jnp.where(tcol // SLOT % NP == trow // TOK, 1.0, 0.0)
        right = jnp.where(nt_dot(rank, pick) == (tcol % SLOT).astype(F32), 1.0, 0.0)
        wcomb[b] = (here * right).astype(BF)

    def s_copy(b):
        sec = down_sec if b == 0 else up_sec
        return remote(sown.at[b], snext.at[b], s_ss.at[b], s_rs.at[b], at(sec, z, p))

    for b in range(2):
        s_copy(b).start()

    mine = z % NH

    def di_copy(k):
        return remote(dinit.at[k], rin.at[0, mine, 0, place(k)], di_ss.at[k], d_rs.at[0, mine, place(k)], zpeer(k))

    @pl.when(outer)
    def _():
        loop(NP - 1, tok_wait)
        xb = xin[...].reshape(PT, FS).astype(BF)
        xres[0] = xb
        sel = jnp.where(s == 0, sown[0, :, 0:PT], sown[1, :, 0:PT])
        picked = jnp.dot(sel, xb, preferred_element_type=F32).astype(BF)
        dinit[...] = picked.reshape(NZ, BLK, FS)
        for k in FAR_FIRST[:-1]:
            di_copy(k).start()
        rin[0, mine, 0, place(0)] = picked[0:BLK]

    def job(j, carry):
        b = jnp.where(low, j, 1 - j)
        step = 1 - 2 * b
        initial = outer & (j == 0)
        to = s + step
        has_next = (to >= 0) & (to < NS)
        to = jnp.clip(to, 0, NS - 1)
        jn = jnp.where(to < NS // 2, b, 1 - b)
        came = jnp.where(initial, s, jnp.clip(s - step, 0, NS - 1))

        def offset(h, m):
            return jnp.where(mine == h, OFFSETS[0][m], OFFSETS[1][m])

        def d_wait(h, m):
            here = rin.at[j, h, 0, m]
            remote(here, here, di_ss.at[m], d_rs.at[j, h, m], zpeer(4)).wait_recv()

        def ag_copy(h, d, m):
            return remote(
                rin.at[j, h, 0, m], rin.at[j, h, d, m], ag_ss.at[j, h, d - 1, m], ag_rs.at[j, h, d - 1, m], xpeer(d)
            )

        def relay(h):
            for m in range(NB):
                if OFFSETS[0][m] == 0:

                    @pl.when(jnp.logical_not(initial & (mine == h)))
                    def _():
                        d_wait(h, m)
                else:
                    d_wait(h, m)
                for d in (2, 1, 3):
                    ag_copy(h, d, m).start()

        for h in range(NH):
            relay(h)

        @pl.when(j == 0)
        def _():
            cps = local_weights()
            cps[0].wait()
            cps[1].wait()
            cps = sibling_weights()
            cps[0].wait_recv()
            cps[1].wait_recv()

        wide, hid = 2 * NC * PIECE, NC * PIECE

        def slice_product(h, d):
            q = (x + NX - d) % NX
            rows = rin[j, h, d].reshape(HROWS, FS).astype(F32)
            g = gain_ref[:, pl.ds(pl.multiple_of(c * HALF + q * FS, 128), FS)].astype(F32)
            ss = jnp.sum(rows * rows, axis=1, keepdims=True)
            u = (rows * g).astype(BF)
            at_row = pl.ds(pl.multiple_of(q * FS, 128), FS)
            for n, w in enumerate((wg, wu)):
                for o in range(NC):
                    sl = slice((n * NC + o) * PIECE, (n * NC + o + 1) * PIECE)
                    part = jnp.dot(u, w[o, at_row, :], preferred_element_type=F32)
                    acc[:, sl] = acc[:, sl] + part if d else part
            ss = jnp.broadcast_to(ss, (HROWS, 128))
            ssq[...] = ssq[...] + ss if d else ss

        def p_copy(h, d, g):
            ks = pl.ds(g * GRP, GRP)
            return remote(
                pout.at[j, h, d - 1, ks], pin.at[j, h, d - 1, ks], p_ss.at[j, h, d - 1, g], p_rs.at[j, h, d - 1, g], xpeer(d)
            )

        def expert(h):
            slice_product(h, 0)
            for d in (1, 3, 2):
                for m in range(NB):
                    ag_copy(h, d, m).wait_recv()
                slice_product(h, d)

            guout[j, h, :, 0:wide] = acc[...].astype(BF)
            ss = ssq[...]
            hi = ss.astype(BF)
            lo = (ss - hi.astype(F32)).astype(BF)
            lanes = lax.broadcasted_iota(jnp.int32, (HROWS, 128), 1)
            guout[j, h, :, wide:] = jnp.where(lanes == 0, hi, lo)
            gu = remote(guout.at[j, h], guin.at[j, h], gu_ss.at[j, h], gu_rs.at[j, h], sib)
            gu.start()
            gu.wait_recv()
            ss = ss[:, 0:1] + guin[j, h, :, wide : wide + 1].astype(F32) + guin[j, h, :, wide + 1 : wide + 2].astype(F32)
            scale = lax.rsqrt(ss * (1.0 / D) + 1e-06)
            gate = (acc[:, 0:hid] + guin[j, h, :, 0:hid].astype(F32)) * scale
            upv = (acc[:, hid:wide] + guin[j, h, :, hid:wide].astype(F32)) * scale
            act[...] = (gate / (1.0 + jnp.exp(-gate)) * upv).astype(BF)

            if h == 0:

                @pl.when(j == 0)
                def _():
                    for cp in local_weights()[2:]:
                        cp.wait()
                    for cp in sibling_weights()[2:]:
                        cp.wait_recv()

            for d in (2, 1, 3):
                part = jnp.dot(act[...], wd[(x + d) % NX], preferred_element_type=F32)
                pout[j, h, d - 1] = part.astype(BF).reshape(NB, BLK, FS)
                for g in range(NB // GRP):
                    p_copy(h, d, g).start()
            pown[h] = jnp.dot(act[...], wd[x], preferred_element_type=F32).reshape(NB, BLK, FS)

        for h in range(NH):
            expert(h)

        def r_copy(h, m, k):
            kk = (NZ - k) % NZ
            return remote(ret.at[j, h, m], retin.at[j, kk], r_ss.at[j, h, m], r_rs.at[j, kk], zpeer(k))

        def give_back(h):
            for g in range(NB // GRP):
                for d in (1, 3, 2):
                    p_copy(h, d, g).wait_recv()
                for m in range(g * GRP, (g + 1) * GRP):
                    total = pown[h, m]
                    for d in (1, 2, 3):
                        total = total + pin[j, h, d - 1, m].astype(F32)
                    total = total.astype(BF)
                    k = offset(h, m)
                    if OFFSETS[0][m]:
                        ret[j, h, m] = total
                        r_copy(h, m, k).start()
                    else:

                        @pl.when(mine == h)
                        def _():
                            retin[j, 0] = total

                        @pl.when(mine != h)
                        def _():
                            ret[j, h, m] = total
                            r_copy(h, m, k).start()

        def x_copy():
            return remote(xnew.at[j], xres.at[jn], x_ss.at[j], x_rs.at[jn], at(to, z, p))

        def st_copy(r):
            return remote(
                st_out.at[j, (p + r + 1) % NP], st_in.at[j, p], st_ss.at[j, r], st_rs.at[j, r], plane(r + 1)
            )

        def owner():
            @pl.when(jnp.logical_not(initial))
            def _():
                remote(xres.at[j], xres.at[j], x_ss.at[j], x_rs.at[j], at(came, z, p)).wait_recv()

            @pl.when(j == 0)
            def _():
                for b_ in range(2):
                    s_copy(b_).wait_recv()

            for k in range(1, NZ):
                remote(retin.at[j, k], retin.at[j, k], r_ss.at[j, 0, 0], r_rs.at[j, k], zpeer(4)).wait_recv()
            back = retin[j].reshape(ROWS, FS)
            branch = jnp.dot(wcomb[b], back, preferred_element_type=F32)
            fresh = (xres[j].astype(F32) + branch).astype(BF)

            @pl.when(has_next)
            def _():
                picked = jnp.dot(snext[b, :, 0:PT], fresh, preferred_element_type=F32).astype(BF)
                dout[j] = picked.reshape(NZ, BLK, FS)
                for k in FAR_FIRST:
                    remote(
                        dout.at[j, k], rin.at[jn, mine, 0, place(k)], d_ss.at[j, k], d_rs.at[jn, mine, place(k)],
                        at(to, (z + k) % NZ, p),
                    ).start()
                xnew[j] = fresh
                x_copy().start()

            st_out[j] = fresh.astype(F32).reshape(NP, TOK, FS)
            st_in[j, p] = st_out[j, p]
            loop(NP - 1, lambda r: st_copy(r).start())

        for h in range(NH):
            give_back(h)
        owner()

        return carry

    lax.fori_loop(0, 2, job, 0)

    def st_wait(n):
        j, r = n // (NP - 1), n % (NP - 1)
        q = (p + NP - r - 1) % NP
        remote(st_out.at[j, q], st_in.at[j, q], st_ss.at[j, r], st_rs.at[j, r], plane(r + 1)).wait()

    loop(2 * (NP - 1), st_wait)
    jf = jnp.where(low, 0, 1)
    for q in range(NP):
        f = (q % NC) * NX + q // NC
        outf_ref[0, :, f * FS : (f + 1) * FS] = st_in[jf, q].astype(BF)
        outr_ref[0, :, f * FS : (f + 1) * FS] = st_in[1 - jf, q].astype(BF)

    loop(NP - 1, lambda r: t_copy(r).wait_send())
    for b in range(2):
        s_copy(b).wait_send()
    for cp in sibling_weights():
        cp.wait_send()

    @pl.when(outer)
    def _():
        loop(NP - 1, lambda r: tok_copy(r).wait_send())
        for k in range(1, NZ):
            di_copy(k).wait_send()

    def drain(j):
        b = jnp.where(low, j, 1 - j)
        to = s + 1 - 2 * b

        @pl.when((to >= 0) & (to < NS))
        def _():
            for k in range(NZ):
                remote(dout.at[j, k], dout.at[j, k], d_ss.at[j, k], d_rs.at[j, 0, 0], zpeer(4)).wait_send()
            remote(xnew.at[j], xnew.at[j], x_ss.at[j], x_rs.at[j], zpeer(4)).wait_send()

        for h in range(NH):
            for m in range(NB):
                for d in (1, 2, 3):
                    here = rin.at[j, h, 0, m]
                    remote(here, here, ag_ss.at[j, h, d - 1, m], ag_rs.at[j, h, d - 1, m], xpeer(d)).wait_send()

                def back_sent():
                    here = ret.at[j, h, m]
                    remote(here, here, r_ss.at[j, h, m], r_rs.at[j, m], zpeer(4)).wait_send()

                if OFFSETS[0][m]:
                    back_sent()
                else:
                    pl.when(mine != h)(back_sent)
            for d in (1, 2, 3):
                for g in range(NB // GRP):
                    here = pout.at[j, h, d - 1, pl.ds(g * GRP, GRP)]
                    remote(here, here, p_ss.at[j, h, d - 1, g], p_rs.at[j, h, d - 1, g], xpeer(d)).wait_send()
            remote(guout.at[j, h], guin.at[j, h], gu_ss.at[j, h], gu_rs.at[j, h], sib).wait_send()

    loop(2, drain)


def run(tokens_fwd, tokens_rev, routes_fwd, routes_rev, weights_fwd, weights_rev, norm_gain, gate_proj, up_proj, down_proj):
    vmem = pl.BlockSpec(memory_space=pltpu.VMEM)
    hbm = pl.BlockSpec(memory_space=pl.ANY)
    dma = pltpu.SemaphoreType.DMA
    out = jax.ShapeDtypeStruct((1, TOK, D), BF)
    wide = 2 * NC * PIECE
    small = [a[0].T for a in (routes_fwd, routes_rev, weights_fwd, weights_rev)]
    return pl.pallas_call(
        kernel,
        name="moe_pipeline",
        out_shape=(out, out),
        in_specs=[vmem] * 7 + [hbm] * 3,
        out_specs=(vmem, vmem),
        scratch_shapes=[
            pltpu.VMEM((NC, HALF, PIECE), BF),
            pltpu.VMEM((NC, HALF, PIECE), BF),
            pltpu.VMEM((NX, NC * PIECE, FS), BF),
            pltpu.VMEM((NP, 2 * TOK, 128), F32),
            pltpu.VMEM((NP, TOK, FS), F32),
            pltpu.VMEM((NP, TOK, FS), F32),
            pltpu.VMEM((2, ROWS, 128), BF),
            pltpu.VMEM((2, ROWS, 128), BF),
            pltpu.VMEM((2, PT, ROWS), BF),
            pltpu.VMEM((2, NH, NX, NB, BLK, FS), BF),
            pltpu.VMEM((HROWS, wide), F32),
            pltpu.VMEM((HROWS, 128), F32),
            pltpu.VMEM((2, NH, HROWS, wide + 128), BF),
            pltpu.VMEM((2, NH, HROWS, wide + 128), BF),
            pltpu.VMEM((HROWS, NC * PIECE), BF),
            pltpu.VMEM((2, NH, NX - 1, NB, BLK, FS), BF),
            pltpu.VMEM((NH, NB, BLK, FS), F32),
            pltpu.VMEM((2, NH, NX - 1, NB, BLK, FS), BF),
            pltpu.VMEM((2, NH, NB, BLK, FS), BF),
            pltpu.VMEM((2, NZ, BLK, FS), BF),
            pltpu.VMEM((2, NZ, BLK, FS), BF),
            pltpu.VMEM((NZ, BLK, FS), BF),
            pltpu.VMEM((2, PT, FS), BF),
            pltpu.VMEM((2, PT, FS), BF),
            pltpu.VMEM((2, NP, TOK, FS), F32),
            pltpu.VMEM((2, NP, TOK, FS), F32),
            dma((NP - 1,)), dma((NP - 1,)), dma((NP - 1,)), dma((NP - 1,)), dma((2,)), dma((2,)),
            dma((2 + NX,)), dma((2 + NX,)), dma((2 + NX,)),
            dma((2, NZ)), dma((2, NH, NB)), dma((NZ,)),
            dma((2, NH, NX - 1, NB)), dma((2, NH, NX - 1, NB)), dma((2, NH)), dma((2, NH)),
            dma((2, NH, NX - 1, NB // GRP)), dma((2, NH, NX - 1, NB // GRP)), dma((2, NH, NB)), dma((2, NZ)),
            dma((2,)), dma((2,)), dma((2, NP - 1)), dma((2, NP - 1)),
        ],
        compiler_params=pltpu.CompilerParams(
            collective_id=0, has_side_effects=True, vmem_limit_bytes=56 * 2**20
        ),
    )(tokens_fwd, tokens_rev, *small, norm_gain, gate_proj, up_proj, down_proj)


def solution(mesh):
    placed = (
        P("expert", None),
        P("expert", None),
        P("section", "expert", None),
        P("section", "expert", None),
        P("section", "expert", None),
        P("section", "expert", None),
        P("section", None),
        P("section", None, "expert"),
        P("section", None, "expert"),
        P("section", "expert", None),
    )
    return jax.shard_map(
        run,
        mesh=mesh,
        in_specs=placed,
        out_specs=(P("section", "expert", None), P("section", "expert", None)),
        check_vma=False,
    )
```

```python
import functools

import jax
import jax.numpy as jnp
from jax import lax
from jax.experimental import pallas as pl
from jax.experimental.pallas import tpu as pltpu
from jax.sharding import PartitionSpec as P

MESH = pl.DeviceIdType.MESH
NS, NZ, NX, NC = 4, 8, 4, 2
NP = NX * NC
TOK = 8
LIVE = NZ
TOPK = 2
SLOT = 2
D = 7168
PIECE = 256
FS = D // NP
HALF = D // NC
ROWS = NZ * NP * SLOT
BLK = NP * SLOT
PT = NP * TOK
NH = 2
NB = NZ // NH
HROWS = ROWS // NH
OFFSETS = ((4, 2, 6, 0), (3, 5, 1, 7))
FAR_FIRST = (4, 3, 5, 2, 6, 1, 7, 0)
GRP = 1
BF, F32 = jnp.bfloat16, jnp.float32


def place(k):
    return OFFSETS[k % NH].index(-k % NZ)


def nt_dot(a, b):
    return lax.dot_general(a, b, (((1,), (1,)), ((), ())), preferred_element_type=F32)


def kernel(
    tokf_hbm, tokr_hbm, rf_hbm, rr_hbm, wf_hbm, wr_hbm, gain_hbm, gate_hbm, up_hbm, down_hbm,
    out_ref,
    tok_ref, rf_ref, rr_ref, wf_ref, wr_ref, gain_ref, out_f32, in_s,
    wg, wu, wd, wall, tall, tokx, xin, sown, wcomb, wbefore, rin, acc, ssq, guout, guin, act, actin,
    pout, pown, pin, ret, retin, dout, xcur, xres, xback, st_out, st_in,
    t_ss, t_rs, tok_ss, tok_rs, s_ss, s_rs, wl_s, w_ss, w_rs, wa_l, wa_ss, wa_rs, a_ss, a_rs,
    d_ss, d_rs, ag_ss, ag_rs, gu_ss, gu_rs, p_ss, p_rs, r_ss, r_rs, x_ss, x_rs, xb_ss, xb_rs, st_ss, st_rs,
):
    s = lax.axis_index("section")
    i = lax.axis_index("expert")
    z, p = i // NP, i % NP
    x, c = p // NC, p % NC
    outer = (s == 0) | (s == NS - 1)
    low = s < NS // 2

    def at(sec, zz, pp):
        return (sec, zz * NP + pp)

    def plane(r):
        return at(s, z, (p + r) % NP)

    def xpeer(d):
        return at(s, z, ((x + d) % NX) * NC + c)

    def zpeer(k):
        return at(s, (z + k) % NZ, p)

    sib = at(s, z, x * NC + 1 - c)
    up_sec, down_sec = (s + 1) % NS, (s + NS - 1) % NS

    def remote(src, dst, ss, rs, dev):
        return pltpu.make_async_remote_copy(
            src_ref=src, dst_ref=dst, send_sem=ss, recv_sem=rs, device_id=dev, device_id_type=MESH
        )

    def loop(n, f):
        def step(n_, carry):
            f(n_)
            return carry

        lax.fori_loop(0, n, step, 0)

    small = [
        pltpu.make_async_copy(src, dst, in_s.at[n])
        for n, (src, dst) in enumerate(
            ((rf_hbm, rf_ref), (rr_hbm, rr_ref), (wf_hbm, wf_ref), (wr_hbm, wr_ref), (gain_hbm, gain_ref))
        )
    ]
    for cp in small:
        cp.start()
    tokens = [pltpu.make_async_copy(src, tok_ref, in_s.at[5]) for src in (tokf_hbm, tokr_hbm)]
    pl.when(s == 0)(lambda: tokens[0].start())
    pl.when(s == NS - 1)(lambda: tokens[1].start())
    bar = pltpu.get_barrier_semaphore()

    def greet(dev):
        pl.semaphore_signal(bar, inc=1, device_id=dev, device_id_type=MESH)

    loop(NP - 1, lambda r: greet(plane(r + 1)))
    loop(NZ - 1, lambda k: greet(zpeer(k + 1)))
    loop(NZ, lambda k: greet(at(up_sec, (z + k) % NZ, p)))
    loop(NZ, lambda k: greet(at(down_sec, (z + k) % NZ, p)))

    def half(core):
        return pl.ds(core * HALF, HALF)

    def slice_of(xx, core):
        return pl.ds(pl.multiple_of(core * HALF + xx * FS, 128), FS)

    def local_gate_up():
        return [
            pltpu.make_async_copy(gate_hbm.at[0, half(c), :], wg.at[c], wl_s.at[0]),
            pltpu.make_async_copy(up_hbm.at[0, half(c), :], wu.at[c], wl_s.at[1]),
        ]

    def sibling_gate_up():
        return [
            remote(gate_hbm.at[0, half(1 - c), :], wg.at[c], w_ss.at[0], w_rs.at[0], sib),
            remote(up_hbm.at[0, half(1 - c), :], wu.at[c], w_ss.at[1], w_rs.at[1], sib),
        ]

    def local_down(q):
        return pltpu.make_async_copy(
            down_hbm.at[0, :, slice_of(q, c)], wd.at[q, pl.ds(c * PIECE, PIECE), :], wl_s.at[2 + q]
        )

    def sibling_down(q):
        return remote(
            down_hbm.at[0, :, slice_of(q, 1 - c)], wd.at[q, pl.ds(c * PIECE, PIECE), :], w_ss.at[2 + q], w_rs.at[2 + q], sib
        )

    def local_spread():
        return pltpu.make_async_copy(down_hbm.at[0, :, slice_of(x, c)], wall.at[p], wa_l.at[0])

    def spread(r):
        q = (p + r + 1) % NP
        return remote(down_hbm.at[0, :, slice_of(q // NC, q % NC)], wall.at[p], wa_ss.at[0], wa_rs.at[0], plane(r + 1))

    def all_spread():
        some = wall.at[pl.ds(0, NP - 1)]
        return remote(some, some, wa_ss.at[0], wa_rs.at[0], sib)

    def start_spread():
        local_spread().start()
        loop(NP - 1, lambda r: spread(r).start())

    def wait_spread():
        local_spread().wait()
        all_spread().wait_recv()

    for cp in local_gate_up():
        cp.start()

    @pl.when(outer)
    def _():
        for q in range(NX):
            local_down(q).start()

    for cp in small:
        cp.wait()
    ei = lax.broadcasted_iota(jnp.int32, (2 * LIVE, TOK), 0)
    eye = jnp.where(
        lax.broadcasted_iota(jnp.int32, (TOK, TOK), 0) == lax.broadcasted_iota(jnp.int32, (TOK, TOK), 1), 1.0, 0.0
    )
    for b, (routes, weights) in enumerate(((rf_ref, wf_ref), (rr_ref, wr_ref))):
        turned = jnp.zeros((2 * LIVE, TOK), F32)
        for n in range(TOPK):
            route, weight = routes[n : n + 1, :], weights[n : n + 1, :].astype(F32)
            turned += jnp.where(route == ei, 1.0, 0.0) + jnp.where(route == ei - LIVE, weight, 0.0)
        tall[p, b * TOK : (b + 1) * TOK, :] = jnp.zeros((TOK, 128), F32)
        tall[p, b * TOK : (b + 1) * TOK, 0 : 2 * LIVE] = nt_dot(eye, turned)

    @pl.when(outer)
    def _():
        tokens[0].wait()
        for q in range(NP):
            f = (q % NC) * NX + q // NC
            sl = slice(f * FS, (f + 1) * FS)
            tokx[q] = tok_ref[:, sl].astype(F32)

    pl.semaphore_wait(bar, NP - 1 + NZ - 1 + 2 * NZ)

    def t_copy(r):
        return remote(tall.at[p], tall.at[p], t_ss.at[0], t_rs.at[0], plane(r + 1))

    few = pl.ds(0, NP - 1)

    def tok_copy(r):
        return remote(tokx.at[(p + r + 1) % NP], xin.at[p], tok_ss.at[0], tok_rs.at[0], plane(r + 1))

    loop(NP - 1, lambda r: t_copy(r).start())

    @pl.when(outer)
    def _():
        loop(NP - 1, lambda r: tok_copy(r).start())

    for cp in sibling_gate_up():
        cp.start()

    @pl.when(outer)
    def _():
        for q in range(NX):
            sibling_down(q).start()

    pl.when(jnp.logical_not(outer))(start_spread)

    @pl.when(outer)
    def _():
        xin[p] = tokx[p]

    remote(tall.at[few], tall.at[few], t_ss.at[0], t_rs.at[0], sib).wait_recv()

    row = lax.broadcasted_iota(jnp.int32, (ROWS, 128), 0)
    col = lax.broadcasted_iota(jnp.int32, (ROWS, 128), 1)
    pick = jnp.where(col == (z + row // BLK) % NZ, 1.0, 0.0)
    pick_w = jnp.where(col - NZ == (z + row // BLK) % NZ, 1.0, 0.0)
    ti = lax.broadcasted_iota(jnp.int32, (PT, PT), 0)
    tj = lax.broadcasted_iota(jnp.int32, (PT, PT), 1)
    before = jnp.where((ti // TOK == tj // TOK) & (tj < ti), 1.0, 0.0)
    srow = lax.broadcasted_iota(jnp.int32, (ROWS, PT), 0)
    scol = lax.broadcasted_iota(jnp.int32, (ROWS, PT), 1)
    trow = lax.broadcasted_iota(jnp.int32, (PT, ROWS), 0)
    tcol = lax.broadcasted_iota(jnp.int32, (PT, ROWS), 1)
    for b in range(2):
        t = tall[:, b * TOK : (b + 1) * TOK, :].reshape(PT, 128)
        rank = jnp.dot(before, t, preferred_element_type=F32)
        here = nt_dot(pick, t) * jnp.where(srow // SLOT % NP == scol // TOK, 1.0, 0.0)
        right = jnp.where(nt_dot(pick, rank) == (srow % SLOT).astype(F32), 1.0, 0.0)
        sown[b, :, 0:PT] = (here * right).astype(BF)
        sown[b, :, PT:128] = jnp.zeros((ROWS, 128 - PT), BF)
        here = nt_dot(t, pick_w) * jnp.where(tcol // SLOT % NP == trow // TOK, 1.0, 0.0)
        right = jnp.where(nt_dot(rank, pick) == (tcol % SLOT).astype(F32), 1.0, 0.0)
        wcomb[b] = (here * right).astype(BF)

    def w_copy(b):
        sec = up_sec if b == 0 else down_sec
        return remote(wcomb.at[b], wbefore.at[b], s_ss.at[b], s_rs.at[b], at(sec, z, p))

    for b in range(2):
        w_copy(b).start()

    @pl.when(outer)
    def _():
        remote(tokx.at[few], xin.at[few], tok_ss.at[0], tok_rs.at[0], sib).wait_recv()
        xcur[0] = xin[...].reshape(PT, FS).astype(BF)

    mine = z % NH

    def st_copy(j, r):
        return remote(
            st_out.at[j, (p + r + 1) % NP], st_in.at[j, p], st_ss.at[j], st_rs.at[j], plane(r + 1)
        )

    def stash(j, value):
        st_out[j] = value.astype(F32).reshape(NP, TOK, FS)
        st_in[j, p] = st_out[j, p]
        loop(NP - 1, lambda r: st_copy(j, r).start())

    def finish(j):
        remote(st_out.at[j, few], st_in.at[j, few], st_ss.at[j], st_rs.at[j], sib).wait_recv()
        for q in range(NP):
            f = (q % NC) * NX + q // NC
            out_f32[j, :, f * FS : (f + 1) * FS] = st_in[j, q]

    def stash_back(j):
        remote(xback.at[j], xback.at[j], xb_ss.at[j], xb_rs.at[j], zpeer(4)).wait_recv()
        stash(j, xback[j])

    def w_wait():
        for b in range(2):
            w_copy(b).wait_recv()

    def job(j, carry):
        b = jnp.where(low, j, 1 - j)
        step = 1 - 2 * b
        initial = outer & (j == 0)
        to = s + step
        has_next = (to >= 0) & (to < NS)
        to = jnp.clip(to, 0, NS - 1)
        jn = jnp.where(to < NS // 2, b, 1 - b)
        came = jnp.clip(s - step, 0, NS - 1)
        jc = jnp.where(came < NS // 2, b, 1 - b)
        dest, slot = jnp.where(has_next, to, s), jnp.where(has_next, jn, 2)

        @pl.when(jnp.logical_not(initial))
        def _():
            pl.when(j == 0)(w_wait)
            remote(xres.at[j], xres.at[j], x_ss.at[j], x_rs.at[j], zpeer(4)).wait_recv()
            remote(retin.at[j], retin.at[j], r_ss.at[j, 0], r_rs.at[j], zpeer(4)).wait_recv()
            branch = jnp.dot(wbefore[b], retin[j].reshape(ROWS, FS), preferred_element_type=F32)
            xcur[j] = (xres[j].astype(F32) + branch).astype(BF)

        picked = jnp.dot(sown[b, :, 0:PT], xcur[j], preferred_element_type=F32).astype(BF)
        dout[j] = picked.reshape(NZ, BLK, FS)
        for k in FAR_FIRST[:-1]:
            remote(
                dout.at[j, k], rin.at[j, mine, 0, place(k)], d_ss.at[j], d_rs.at[j, mine, place(k)], zpeer(k)
            ).start()
        rin[j, mine, 0, place(0)] = picked[0:BLK]

        @pl.when(has_next)
        def _():
            remote(xcur.at[j], xres.at[jn], x_ss.at[j], x_rs.at[jn], at(to, z, p)).start()

        @pl.when(jnp.logical_not(initial))
        def _():
            remote(xcur.at[j], xback.at[jc], xb_ss.at[j], xb_rs.at[jc], at(came, z, p)).start()

        def offset(h, m):
            return jnp.where(mine == h, OFFSETS[0][m], OFFSETS[1][m])

        def d_wait(h, m):
            here = rin.at[j, h, 0, m]
            remote(here, here, d_ss.at[j], d_rs.at[j, h, m], zpeer(4)).wait_recv()

        def ag_copy(h, d, m):
            return remote(
                rin.at[j, h, 0, m], rin.at[j, h, d, m], ag_ss.at[j, h, d - 1], ag_rs.at[j, h, d - 1], xpeer(d)
            )

        def relay(h):
            for m in range(NB):
                if OFFSETS[0][m] == 0:

                    @pl.when(mine != h)
                    def _():
                        d_wait(h, m)
                else:
                    d_wait(h, m)
                for d in (2, 1, 3):
                    ag_copy(h, d, m).start()

        for h in range(NH):
            relay(h)

        @pl.when(j == 0)
        def _():
            for cp in local_gate_up():
                cp.wait()
            for cp in sibling_gate_up():
                cp.wait_recv()

        wide, hid = 2 * NC * PIECE, NC * PIECE

        def slice_product(h, d):
            q = (x + NX - d) % NX
            rows = rin[j, h, d].reshape(HROWS, FS).astype(F32)
            g = gain_ref[:, pl.ds(pl.multiple_of(c * HALF + q * FS, 128), FS)].astype(F32)
            ss = jnp.sum(rows * rows, axis=1, keepdims=True)
            u = (rows * g).astype(BF)
            at_row = pl.ds(pl.multiple_of(q * FS, 128), FS)
            for n, w in enumerate((wg, wu)):
                for o in range(NC):
                    sl = slice((n * NC + o) * PIECE, (n * NC + o + 1) * PIECE)
                    part = jnp.dot(u, w[o, at_row, :], preferred_element_type=F32)
                    acc[:, sl] = acc[:, sl] + part if d else part
            ss = jnp.broadcast_to(ss, (HROWS, 128))
            ssq[...] = ssq[...] + ss if d else ss

        def p_copy(h, d, g):
            ks = pl.ds(g * GRP, GRP)
            return remote(
                pout.at[h, d - 1, ks], pin.at[h, d - 1, ks], p_ss.at[h, d - 1], p_rs.at[h, d - 1, g], xpeer(d)
            )

        def act_copy(h, d):
            return remote(act.at[j, h], actin.at[j, h, d - 1], a_ss.at[j, h, d - 1], a_rs.at[j, h, d - 1], xpeer(d))

        def all_of(value, q):
            w = wall[pl.ds(q * NC, NC)].reshape(NC * PIECE, FS)
            return jnp.dot(value, w, preferred_element_type=F32).reshape(NB, BLK, FS)

        def expert(h):
            slice_product(h, 0)
            for d in (1, 3, 2):
                remote(rin.at[j, h, 0], rin.at[j, h, d], ag_ss.at[j, h, d - 1], ag_rs.at[j, h, d - 1], sib).wait_recv()
                slice_product(h, d)

            guout[j, h, :, 0:wide] = acc[...].astype(BF)
            ss = ssq[...]
            hi = ss.astype(BF)
            lo = (ss - hi.astype(F32)).astype(BF)
            lanes = lax.broadcasted_iota(jnp.int32, (HROWS, 128), 1)
            guout[j, h, :, wide:] = jnp.where(lanes == 0, hi, lo)
            gu = remote(guout.at[j, h], guin.at[j, h], gu_ss.at[j, h], gu_rs.at[j, h], sib)
            gu.start()
            gu.wait_recv()
            ss = ss[:, 0:1] + guin[j, h, :, wide : wide + 1].astype(F32) + guin[j, h, :, wide + 1 : wide + 2].astype(F32)
            scale = lax.rsqrt(ss * (1.0 / D) + 1e-06)
            gate = (acc[:, 0:hid] + guin[j, h, :, 0:hid].astype(F32)) * scale
            upv = (acc[:, hid:wide] + guin[j, h, :, hid:wide].astype(F32)) * scale
            act[j, h] = (gate / (1.0 + jnp.exp(-gate)) * upv).astype(BF)

            @pl.when(initial)
            def _():
                if h == 0:
                    for q in range(NX):
                        local_down(q).wait()
                        sibling_down(q).wait_recv()
                for d in (2, 1, 3):
                    part = jnp.dot(act[j, h], wd[(x + d) % NX], preferred_element_type=F32)
                    pout[h, d - 1] = part.astype(BF).reshape(NB, BLK, FS)
                for g in range(NB // GRP):
                    for d in (2, 1, 3):
                        p_copy(h, d, g).start()
                pown[h] = jnp.dot(act[j, h], wd[x], preferred_element_type=F32).reshape(NB, BLK, FS)

            @pl.when(jnp.logical_not(initial))
            def _():
                for d in (2, 1, 3):
                    act_copy(h, d).start()
                if h == 0:
                    pl.when((j == 0) | outer)(wait_spread)
                pown[h] = all_of(act[j, h], x)

        for h in range(NH):
            expert(h)

        pl.when(j == 1)(lambda: stash_back(0))

        def r_copy(h, m, k):
            kk = (NZ - k) % NZ
            return remote(
                ret.at[j, h, m], retin.at[slot, kk], r_ss.at[j, h], r_rs.at[slot], at(dest, (z + k) % NZ, p)
            )

        def hand(h, m, total):
            k = offset(h, m)
            total = total.astype(BF)
            if OFFSETS[0][m]:
                ret[j, h, m] = total
                r_copy(h, m, k).start()
            else:
                here = (mine == h) & jnp.logical_not(has_next)

                @pl.when(here)
                def _():
                    retin[2, 0] = total

                @pl.when(jnp.logical_not(here))
                def _():
                    ret[j, h, m] = total
                    r_copy(h, m, k).start()

        def give_back(h):
            @pl.when(initial)
            def _():
                for g in range(NB // GRP):
                    for d in (1, 3, 2):
                        p_copy(h, d, g).wait_recv()
                    for m in range(g * GRP, (g + 1) * GRP):
                        total = pown[h, m]
                        for d in (1, 2, 3):
                            total = total + pin[h, d - 1, m].astype(F32)
                        hand(h, m, total)

            @pl.when(jnp.logical_not(initial))
            def _():
                total = pown[h]
                for d in (1, 3, 2):
                    act_copy(h, d).wait_recv()
                    total = total + all_of(actin[j, h, d - 1], (x + NX - d) % NX)
                for m in range(NB):
                    hand(h, m, total[m])

        for h in range(NH):
            give_back(h)
        pl.when(initial)(w_wait)
        pl.when(initial)(start_spread)
        pl.when(j == 1)(lambda: finish(0))

        @pl.when(jnp.logical_not(has_next))
        def _():
            others = retin.at[2, pl.ds(1, NZ - 1)]
            remote(others, others, r_ss.at[j, 0], r_rs.at[2], zpeer(4)).wait_recv()
            branch = jnp.dot(wcomb[b], retin[2].reshape(ROWS, FS), preferred_element_type=F32)
            stash(j, (xcur[j].astype(F32) + branch).astype(BF))

        return carry

    lax.fori_loop(0, 2, job, 0)
    pl.when(jnp.logical_not(outer))(lambda: stash_back(1))

    finish(1)
    jf = jnp.where(low, 0, 1)
    out_ref[0:TOK, :] = out_f32[jf].astype(BF)
    out_ref[TOK : 2 * TOK, :] = out_f32[1 - jf].astype(BF)

    for j in range(2):
        remote(st_out.at[j, few], st_in.at[j, few], st_ss.at[j], st_rs.at[j], sib).wait_send()
    remote(tall.at[few], tall.at[few], t_ss.at[0], t_rs.at[0], sib).wait_send()
    for b in range(2):
        w_copy(b).wait_send()
    for cp in sibling_gate_up():
        cp.wait_send()
    all_spread().wait_send()

    @pl.when(outer)
    def _():
        remote(tokx.at[few], xin.at[few], tok_ss.at[0], tok_rs.at[0], sib).wait_send()
        for q in range(NX):
            sibling_down(q).wait_send()
        for h in range(NH):
            for d in (1, 2, 3):
                here = pout.at[h, d - 1]
                remote(here, here, p_ss.at[h, d - 1], p_rs.at[h, d - 1, 0], xpeer(d)).wait_send()

    def drain(j):
        b = jnp.where(low, j, 1 - j)
        to = s + 1 - 2 * b
        has_next = (to >= 0) & (to < NS)

        sent = dout.at[j, pl.ds(1, NZ - 1)]
        remote(sent, sent, d_ss.at[j], d_rs.at[j, 0, 0], zpeer(4)).wait_send()

        @pl.when(has_next)
        def _():
            remote(xcur.at[j], xcur.at[j], x_ss.at[j], x_rs.at[j], zpeer(4)).wait_send()

        @pl.when(jnp.logical_not(outer & (j == 0)))
        def _():
            remote(xcur.at[j], xcur.at[j], xb_ss.at[j], xb_rs.at[j], zpeer(4)).wait_send()

        for h in range(NH):
            for d in (1, 2, 3):
                here = rin.at[j, h, 0]
                remote(here, here, ag_ss.at[j, h, d - 1], ag_rs.at[j, h, d - 1], xpeer(d)).wait_send()

            here, fewer = ret.at[j, h], ret.at[j, h, pl.ds(0, NB - 1)]
            whole = (mine != h) | has_next
            pl.when(whole)(lambda: remote(here, here, r_ss.at[j, h], r_rs.at[j], zpeer(4)).wait_send())
            pl.when(jnp.logical_not(whole))(lambda: remote(fewer, fewer, r_ss.at[j, h], r_rs.at[j], zpeer(4)).wait_send())

            @pl.when(jnp.logical_not(outer & (j == 0)))
            def _():
                for d in (1, 2, 3):
                    here = act.at[j, h]
                    remote(here, here, a_ss.at[j, h, d - 1], a_rs.at[j, h, d - 1], xpeer(d)).wait_send()

            remote(guout.at[j, h], guin.at[j, h], gu_ss.at[j, h], gu_rs.at[j, h], sib).wait_send()

    loop(2, drain)


def split(both_ref, outf_ref, outr_ref):
    outf_ref[0] = both_ref[0:TOK, :]
    outr_ref[0] = both_ref[TOK : 2 * TOK, :]


def run(tokens_fwd, tokens_rev, routes_fwd, routes_rev, weights_fwd, weights_rev, norm_gain, gate_proj, up_proj, down_proj):
    vmem = pl.BlockSpec(memory_space=pltpu.VMEM)
    hbm = pl.BlockSpec(memory_space=pl.ANY)
    dma = pltpu.SemaphoreType.DMA
    out = jax.ShapeDtypeStruct((2 * TOK, D), BF)
    wide = 2 * NC * PIECE
    small = [a[0].T for a in (routes_fwd, routes_rev, weights_fwd, weights_rev)]
    both = pl.pallas_call(
        kernel,
        name="moe_pipeline",
        out_shape=out,
        in_specs=[hbm] * 10,
        out_specs=vmem,
        scratch_shapes=[
            pltpu.VMEM((TOK, D), BF),
            pltpu.VMEM((TOPK, TOK), jnp.int32),
            pltpu.VMEM((TOPK, TOK), jnp.int32),
            pltpu.VMEM((TOPK, TOK), BF),
            pltpu.VMEM((TOPK, TOK), BF),
            pltpu.VMEM((1, D), BF),
            pltpu.VMEM((2, TOK, D), F32),
            dma((6,)),
            pltpu.VMEM((NC, HALF, PIECE), BF),
            pltpu.VMEM((NC, HALF, PIECE), BF),
            pltpu.VMEM((NX, NC * PIECE, FS), BF),
            pltpu.VMEM((NP, PIECE, FS), BF),
            pltpu.VMEM((NP, 2 * TOK, 128), F32),
            pltpu.VMEM((NP, TOK, FS), F32),
            pltpu.VMEM((NP, TOK, FS), F32),
            pltpu.VMEM((2, ROWS, 128), BF),
            pltpu.VMEM((2, PT, ROWS), BF),
            pltpu.VMEM((2, PT, ROWS), BF),
            pltpu.VMEM((2, NH, NX, NB, BLK, FS), BF),
            pltpu.VMEM((HROWS, wide), F32),
            pltpu.VMEM((HROWS, 128), F32),
            pltpu.VMEM((2, NH, HROWS, wide + 128), BF),
            pltpu.VMEM((2, NH, HROWS, wide + 128), BF),
            pltpu.VMEM((2, NH, HROWS, NC * PIECE), BF),
            pltpu.VMEM((2, NH, NX - 1, HROWS, NC * PIECE), BF),
            pltpu.VMEM((NH, NX - 1, NB, BLK, FS), BF),
            pltpu.VMEM((NH, NB, BLK, FS), F32),
            pltpu.VMEM((NH, NX - 1, NB, BLK, FS), BF),
            pltpu.VMEM((2, NH, NB, BLK, FS), BF),
            pltpu.VMEM((3, NZ, BLK, FS), BF),
            pltpu.VMEM((2, NZ, BLK, FS), BF),
            pltpu.VMEM((2, PT, FS), BF),
            pltpu.VMEM((2, PT, FS), BF),
            pltpu.VMEM((2, PT, FS), BF),
            pltpu.VMEM((2, NP, TOK, FS), F32),
            pltpu.VMEM((2, NP, TOK, FS), F32),
            dma((1,)), dma((1,)), dma((1,)), dma((1,)), dma((2,)), dma((2,)),
            dma((2 + NX,)), dma((2 + NX,)), dma((2 + NX,)),
            dma((1,)), dma((1,)), dma((1,)), dma((2, NH, NX - 1)), dma((2, NH, NX - 1)),
            dma((2,)), dma((2, NH, NB)),
            dma((2, NH, NX - 1)), dma((2, NH, NX - 1)), dma((2, NH)), dma((2, NH)),
            dma((NH, NX - 1)), dma((NH, NX - 1, NB // GRP)), dma((2, NH)), dma((3,)),
            dma((2,)), dma((2,)), dma((2,)), dma((2,)), dma((2,)), dma((2,)),
        ],
        compiler_params=pltpu.CompilerParams(
            collective_id=0, has_side_effects=True, vmem_limit_bytes=56 * 2**20
        ),
    )(tokens_fwd, tokens_rev, *small, norm_gain, gate_proj, up_proj, down_proj)
    one = jax.ShapeDtypeStruct((1, TOK, D), BF)
    return pl.pallas_call(
        split, name="split", out_shape=(one, one), in_specs=[vmem], out_specs=(vmem, vmem)
    )(both)


def solution(mesh):
    placed = (
        P("expert", None),
        P("expert", None),
        P("section", "expert", None),
        P("section", "expert", None),
        P("section", "expert", None),
        P("section", "expert", None),
        P("section", None),
        P("section", None, "expert"),
        P("section", None, "expert"),
        P("section", "expert", None),
    )
    return jax.shard_map(
        run,
        mesh=mesh,
        in_specs=placed,
        out_specs=(P("section", "expert", None), P("section", "expert", None)),
        check_vma=False,
    )
```

```python
import functools

import jax
import jax.numpy as jnp
from jax import lax
from jax.experimental import pallas as pl
from jax.experimental.pallas import tpu as pltpu
from jax.sharding import PartitionSpec as P

MESH = pl.DeviceIdType.MESH
NS, NZ, NX, NC = 4, 8, 4, 2
NP = NX * NC
TOK = 8
LIVE = NZ
TOPK = 2
SLOT = 2
D = 7168
PIECE = 256
FS = D // NP
HALF = D // NC
ROWS = NZ * NP * SLOT
BLK = NP * SLOT
PT = NP * TOK
HALFWAY = 512
NH = 2
NB = NZ // NH
HROWS = ROWS // NH
GROWS = HROWS // 2
OFFSETS = ((0, 2, 6, 4), (1, 7, 3, 5))
NEAR_FIRST = (1, 7, 2, 6, 3, 5, 4)
FAR_BLOCKS = (3, 1, 2, 0)
BF, F32 = jnp.bfloat16, jnp.float32


def place(k):
    return OFFSETS[k % NH].index(-k % NZ)


def pack(value):
    return jnp.concatenate([value[:, 0:HALFWAY], value[:, FS - HALFWAY : FS]], axis=0).astype(BF)


def unpack(packed, ref, start):
    value = packed.astype(F32)
    ref[:, start : start + HALFWAY] = value[0:TOK]
    ref[:, start + FS - HALFWAY : start + FS] = value[TOK : 2 * TOK]


def nt_dot(a, b):
    return lax.dot_general(a, b, (((1,), (1,)), ((), ())), preferred_element_type=F32)


def kernel(
    tokf_hbm, tokr_hbm, rf_hbm, rr_hbm, wf_hbm, wr_hbm, gain_hbm, gate_hbm, up_hbm, down_hbm,
    out_ref,
    tok_ref, rf_ref, rr_ref, wf_ref, wr_ref, gain_ref, out_f32, in_s,
    wg, wu, wd, wall, tall, tokx, xin, plane32, sown, wcomb, wbefore, rin, acc, ssq, guout, guin, act, actin,
    pout, pown, pin, ret, retin, dout, xcur, xres, xback, st_out, st_in,
    t_ss, t_rs, tok_ss, tok_rs, s_ss, s_rs, wl_s, w_ss, w_rs, wa_l, wa_ss, wa_rs, a_ss, a_rs,
    d_ss, d_rs, ag_ss, ag_rs, gu_ss, gu_rs, p_ss, p_rs, r_ss, r_rs, x_ss, x_rs, xb_ss, xb_rs, st_ss, st_rs,
):
    s = lax.axis_index("section")
    i = lax.axis_index("expert")
    z, p = i // NP, i % NP
    x, c = p // NC, p % NC
    outer = (s == 0) | (s == NS - 1)
    low = s < NS // 2

    def at(sec, zz, pp):
        return (sec, zz * NP + pp)

    def plane(r):
        return at(s, z, (p + r) % NP)

    def xpeer(d):
        return at(s, z, ((x + d) % NX) * NC + c)

    def zpeer(k):
        return at(s, (z + k) % NZ, p)

    sib = at(s, z, x * NC + 1 - c)
    up_sec, down_sec = (s + 1) % NS, (s + NS - 1) % NS

    def remote(src, dst, ss, rs, dev):
        return pltpu.make_async_remote_copy(
            src_ref=src, dst_ref=dst, send_sem=ss, recv_sem=rs, device_id=dev, device_id_type=MESH
        )

    def loop(n, f):
        def step(n_, carry):
            f(n_)
            return carry

        lax.fori_loop(0, n, step, 0)

    bar = pltpu.get_barrier_semaphore()

    def greet(dev):
        pl.semaphore_signal(bar, inc=1, device_id=dev, device_id_type=MESH)

    loop(NP - 1, lambda r: greet(plane(r + 1)))
    loop(NZ - 1, lambda k: greet(zpeer(k + 1)))
    loop(NZ, lambda k: greet(at(up_sec, (z + k) % NZ, p)))
    loop(NZ, lambda k: greet(at(down_sec, (z + k) % NZ, p)))

    small = [
        pltpu.make_async_copy(src, dst, in_s.at[n])
        for n, (src, dst) in enumerate(
            ((rf_hbm, rf_ref), (rr_hbm, rr_ref), (wf_hbm, wf_ref), (wr_hbm, wr_ref), (gain_hbm, gain_ref))
        )
    ]
    for cp in small:
        cp.start()
    tokens = [pltpu.make_async_copy(src, tok_ref, in_s.at[5]) for src in (tokf_hbm, tokr_hbm)]
    pl.when(s == 0)(lambda: tokens[0].start())
    pl.when(s == NS - 1)(lambda: tokens[1].start())

    def half(core):
        return pl.ds(core * HALF, HALF)

    def slice_of(xx, core):
        return pl.ds(pl.multiple_of(core * HALF + xx * FS, 128), FS)

    def local_gate_up():
        return [
            pltpu.make_async_copy(gate_hbm.at[0, half(c), :], wg.at[c], wl_s.at[0]),
            pltpu.make_async_copy(up_hbm.at[0, half(c), :], wu.at[c], wl_s.at[1]),
        ]

    def sibling_gate_up():
        return [
            remote(gate_hbm.at[0, half(1 - c), :], wg.at[c], w_ss.at[0], w_rs.at[0], sib),
            remote(up_hbm.at[0, half(1 - c), :], wu.at[c], w_ss.at[1], w_rs.at[1], sib),
        ]

    def local_down(q):
        return pltpu.make_async_copy(
            down_hbm.at[0, :, slice_of(q, c)], wd.at[q, pl.ds(c * PIECE, PIECE), :], wl_s.at[2 + q]
        )

    def sibling_down(q):
        return remote(
            down_hbm.at[0, :, slice_of(q, 1 - c)], wd.at[q, pl.ds(c * PIECE, PIECE), :], w_ss.at[2 + q], w_rs.at[2 + q], sib
        )

    def local_spread():
        return pltpu.make_async_copy(down_hbm.at[0, :, slice_of(x, c)], wall.at[p], wa_l.at[0])

    def spread(r):
        q = (p + r + 1) % NP
        return remote(down_hbm.at[0, :, slice_of(q // NC, q % NC)], wall.at[p], wa_ss.at[0], wa_rs.at[0], plane(r + 1))

    def all_spread():
        some = wall.at[pl.ds(0, NP - 1)]
        return remote(some, some, wa_ss.at[0], wa_rs.at[0], sib)

    def start_spread():
        local_spread().start()
        loop(NP - 1, lambda r: spread(r).start())

    def wait_spread():
        local_spread().wait()
        all_spread().wait_recv()

    for cp in local_gate_up():
        cp.start()

    @pl.when(outer)
    def _():
        for q in range(NX):
            local_down(q).start()

    for cp in small:
        cp.wait()
    ei = lax.broadcasted_iota(jnp.int32, (2 * LIVE, TOK), 0)
    eye = jnp.where(
        lax.broadcasted_iota(jnp.int32, (TOK, TOK), 0) == lax.broadcasted_iota(jnp.int32, (TOK, TOK), 1), 1.0, 0.0
    )
    for b, (routes, weights) in enumerate(((rf_ref, wf_ref), (rr_ref, wr_ref))):
        turned = jnp.zeros((2 * LIVE, TOK), F32)
        for n in range(TOPK):
            route, weight = routes[n : n + 1, :], weights[n : n + 1, :].astype(F32)
            turned += jnp.where(route == ei, 1.0, 0.0) + jnp.where(route == ei - LIVE, weight, 0.0)
        tall[p, b * TOK : (b + 1) * TOK, :] = jnp.zeros((TOK, 128), F32)
        tall[p, b * TOK : (b + 1) * TOK, 0 : 2 * LIVE] = nt_dot(eye, turned)

    @pl.when(outer)
    def _():
        tokens[0].wait()
        for q in range(NP):
            f = (q % NC) * NX + q // NC
            sl = slice(f * FS, (f + 1) * FS)
            tokx[q] = pack(tok_ref[:, sl].astype(F32))

    pl.semaphore_wait(bar, NP - 1 + NZ - 1 + 2 * NZ)

    def t_copy(r):
        return remote(tall.at[p], tall.at[p], t_ss.at[0], t_rs.at[0], plane(r + 1))

    few = pl.ds(0, NP - 1)

    def tok_copy(r):
        return remote(tokx.at[(p + r + 1) % NP], xin.at[p], tok_ss.at[0], tok_rs.at[0], plane(r + 1))

    loop(NP - 1, lambda r: t_copy(r).start())

    @pl.when(outer)
    def _():
        loop(NP - 1, lambda r: tok_copy(r).start())

    for cp in sibling_gate_up():
        cp.start()

    @pl.when(outer)
    def _():
        for q in range(NX):
            sibling_down(q).start()

    pl.when(jnp.logical_not(outer))(start_spread)

    @pl.when(outer)
    def _():
        xin[p] = tokx[p]

    remote(tall.at[few], tall.at[few], t_ss.at[0], t_rs.at[0], sib).wait_recv()

    row = lax.broadcasted_iota(jnp.int32, (ROWS, 128), 0)
    col = lax.broadcasted_iota(jnp.int32, (ROWS, 128), 1)
    pick = jnp.where(col == (z + row // BLK) % NZ, 1.0, 0.0)
    pick_w = jnp.where(col - NZ == (z + row // BLK) % NZ, 1.0, 0.0)
    ti = lax.broadcasted_iota(jnp.int32, (PT, PT), 0)
    tj = lax.broadcasted_iota(jnp.int32, (PT, PT), 1)
    before = jnp.where((ti // TOK == tj // TOK) & (tj < ti), 1.0, 0.0)
    srow = lax.broadcasted_iota(jnp.int32, (ROWS, PT), 0)
    scol = lax.broadcasted_iota(jnp.int32, (ROWS, PT), 1)
    trow = lax.broadcasted_iota(jnp.int32, (PT, ROWS), 0)
    tcol = lax.broadcasted_iota(jnp.int32, (PT, ROWS), 1)
    for b in range(2):
        t = tall[:, b * TOK : (b + 1) * TOK, :].reshape(PT, 128)
        rank = jnp.dot(before, t, preferred_element_type=F32)
        here = nt_dot(pick, t) * jnp.where(srow // SLOT % NP == scol // TOK, 1.0, 0.0)
        right = jnp.where(nt_dot(pick, rank) == (srow % SLOT).astype(F32), 1.0, 0.0)
        sown[b, :, 0:PT] = (here * right).astype(BF)
        sown[b, :, PT:128] = jnp.zeros((ROWS, 128 - PT), BF)
        here = nt_dot(t, pick_w) * jnp.where(tcol // SLOT % NP == trow // TOK, 1.0, 0.0)
        right = jnp.where(nt_dot(rank, pick) == (tcol % SLOT).astype(F32), 1.0, 0.0)
        wcomb[b] = (here * right).astype(BF)

    def w_copy(b):
        sec = up_sec if b == 0 else down_sec
        return remote(wcomb.at[b], wbefore.at[b], s_ss.at[b], s_rs.at[b], at(sec, z, p))

    for b in range(2):
        w_copy(b).start()

    @pl.when(outer)
    def _():
        remote(tokx.at[few], xin.at[few], tok_ss.at[0], tok_rs.at[0], sib).wait_recv()
        for q in range(NP):
            unpack(xin[q], plane32.at[q], 0)
        xcur[0] = plane32[...].reshape(PT, FS).astype(BF)

    mine = z % NH

    def st_copy(j, r):
        return remote(
            st_out.at[j, (p + r + 1) % NP], st_in.at[j, p], st_ss.at[j], st_rs.at[j], plane(r + 1)
        )

    def stash(j, value):
        value = value.astype(F32).reshape(NP, TOK, FS)
        for q in range(NP):
            st_out[j, q] = pack(value[q])
        st_in[j, p] = st_out[j, p]
        loop(NP - 1, lambda r: st_copy(j, r).start())

    def finish(j):
        remote(st_out.at[j, few], st_in.at[j, few], st_ss.at[j], st_rs.at[j], sib).wait_recv()
        for q in range(NP):
            f = (q % NC) * NX + q // NC
            unpack(st_in[j, q], out_f32.at[j], f * FS)

    def stash_back(j):
        remote(xback.at[j], xback.at[j], xb_ss.at[j], xb_rs.at[j], zpeer(4)).wait_recv()
        stash(j, xback[j])

    def w_wait():
        for b in range(2):
            w_copy(b).wait_recv()

    def job(j, carry):
        b = jnp.where(low, j, 1 - j)
        step = 1 - 2 * b
        initial = outer & (j == 0)
        to = s + step
        has_next = (to >= 0) & (to < NS)
        to = jnp.clip(to, 0, NS - 1)
        jn = jnp.where(to < NS // 2, b, 1 - b)
        came = jnp.clip(s - step, 0, NS - 1)
        jc = jnp.where(came < NS // 2, b, 1 - b)
        dest, slot = jnp.where(has_next, to, s), jnp.where(has_next, jn, 2)

        @pl.when(jnp.logical_not(initial))
        def _():
            pl.when(j == 0)(w_wait)
            remote(xres.at[j], xres.at[j], x_ss.at[j], x_rs.at[j], zpeer(4)).wait_recv()
            remote(retin.at[j], retin.at[j], r_ss.at[j, 0], r_rs.at[j], zpeer(4)).wait_recv()
            branch = jnp.dot(wbefore[b], retin[j].reshape(ROWS, FS), preferred_element_type=F32)
            xcur[j] = (xres[j].astype(F32) + branch).astype(BF)

        picked = jnp.dot(sown[b, :, 0:PT], xcur[j], preferred_element_type=F32).astype(BF)
        dout[j] = picked.reshape(NZ, BLK, FS)
        rin[j, mine, 0, place(0)] = picked[0:BLK]
        for k in NEAR_FIRST:
            remote(
                dout.at[j, k], rin.at[j, mine, 0, place(k)], d_ss.at[j], d_rs.at[j, mine, place(k)], zpeer(k)
            ).start()

        @pl.when(has_next)
        def _():
            remote(xcur.at[j], xres.at[jn], x_ss.at[j], x_rs.at[jn], at(to, z, p)).start()

        @pl.when(jnp.logical_not(initial))
        def _():
            remote(xcur.at[j], xback.at[jc], xb_ss.at[j], xb_rs.at[jc], at(came, z, p)).start()

        def offset(h, m):
            return jnp.where(mine == h, OFFSETS[0][m], OFFSETS[1][m])

        def d_wait(h, m):
            here = rin.at[j, h, 0, m]
            remote(here, here, d_ss.at[j], d_rs.at[j, h, m], zpeer(4)).wait_recv()

        def ag_copy(h, d, m):
            return remote(
                rin.at[j, h, 0, m], rin.at[j, h, d, m], ag_ss.at[j, h, d - 1], ag_rs.at[j, h, d - 1], xpeer(d)
            )

        def relay(h):
            for m in range(NB):
                if OFFSETS[0][m] == 0:

                    @pl.when(mine != h)
                    def _():
                        d_wait(h, m)
                else:
                    d_wait(h, m)
                for d in (2, 1, 3):
                    ag_copy(h, d, m).start()

        for h in range(NH):
            relay(h)

        @pl.when(j == 0)
        def _():
            for cp in local_gate_up():
                cp.wait()
            for cp in sibling_gate_up():
                cp.wait_recv()

        wide, hid = 2 * NC * PIECE, NC * PIECE

        def slice_product(h, d):
            q = (x + NX - d) % NX
            rows = rin[j, h, d].reshape(HROWS, FS).astype(F32)
            g = gain_ref[:, pl.ds(pl.multiple_of(c * HALF + q * FS, 128), FS)].astype(F32)
            ss = jnp.sum(rows * rows, axis=1, keepdims=True)
            u = (rows * g).astype(BF)
            at_row = pl.ds(pl.multiple_of(q * FS, 128), FS)
            for n, w in enumerate((wg, wu)):
                for o in range(NC):
                    sl = slice((n * NC + o) * PIECE, (n * NC + o + 1) * PIECE)
                    part = jnp.dot(u, w[o, at_row, :], preferred_element_type=F32)
                    acc[:, sl] = acc[:, sl] + part if d else part
            ss = jnp.broadcast_to(ss, (HROWS, 128))
            ssq[...] = ssq[...] + ss if d else ss

        def p_copy(h, d, g):
            return remote(
                pout.at[h, d - 1, g], pin.at[h, d - 1, g], p_ss.at[h, d - 1], p_rs.at[h, d - 1, g], xpeer(d)
            )

        def act_copy(h, d, g):
            rows = pl.ds(g * GROWS, GROWS)
            return remote(
                act.at[j, h, rows], actin.at[j, h, d - 1, rows], a_ss.at[j, h], a_rs.at[j, h, d - 1, g], xpeer(d)
            )

        def all_of(value, q):
            w = wall[pl.ds(q * NC, NC)].reshape(NC * PIECE, FS)
            return jnp.dot(value, w, preferred_element_type=F32).reshape(-1, BLK, FS)

        def expert(h):
            slice_product(h, 0)
            for d in (1, 3, 2):
                remote(rin.at[j, h, 0], rin.at[j, h, d], ag_ss.at[j, h, d - 1], ag_rs.at[j, h, d - 1], sib).wait_recv()
                slice_product(h, d)

            guout[j, h, :, 0:wide] = acc[...].astype(BF)
            ss = ssq[...]
            hi = ss.astype(BF)
            lo = (ss - hi.astype(F32)).astype(BF)
            lanes = lax.broadcasted_iota(jnp.int32, (HROWS, 128), 1)
            guout[j, h, :, wide:] = jnp.where(lanes == 0, hi, lo)
            gu = remote(guout.at[j, h], guin.at[j, h], gu_ss.at[j, h], gu_rs.at[j, h], sib)
            gu.start()
            gu.wait_recv()
            ss = ss[:, 0:1] + guin[j, h, :, wide : wide + 1].astype(F32) + guin[j, h, :, wide + 1 : wide + 2].astype(F32)
            scale = lax.rsqrt(ss * (1.0 / D) + 1e-06)
            gate = (acc[:, 0:hid] + guin[j, h, :, 0:hid].astype(F32)) * scale
            upv = (acc[:, hid:wide] + guin[j, h, :, hid:wide].astype(F32)) * scale
            act[j, h] = (gate / (1.0 + jnp.exp(-gate)) * upv).astype(BF)

            @pl.when(initial)
            def _():
                if h == 0:
                    for q in range(NX):
                        local_down(q).wait()
                        sibling_down(q).wait_recv()
                for d in (2, 1, 3):
                    part = jnp.dot(act[j, h], wd[(x + d) % NX], preferred_element_type=F32)
                    pout[h, d - 1] = part.astype(BF).reshape(NB, BLK, FS)
                for g in FAR_BLOCKS:
                    for d in (2, 1, 3):
                        p_copy(h, d, g).start()
                pown[h] = jnp.dot(act[j, h], wd[x], preferred_element_type=F32).reshape(NB, BLK, FS)

            @pl.when(jnp.logical_not(initial))
            def _():
                for g in (1, 0):
                    for d in (2, 1, 3):
                        act_copy(h, d, g).start()
                if h == 0:
                    pl.when((j == 0) | outer)(wait_spread)
                pown[h] = all_of(act[j, h], x)

        for h in range(NH):
            expert(h)

        pl.when(j == 1)(lambda: stash_back(0))

        def r_copy(h, m, k):
            kk = (NZ - k) % NZ
            return remote(
                ret.at[j, h, m], retin.at[slot, kk], r_ss.at[j, h], r_rs.at[slot], at(dest, (z + k) % NZ, p)
            )

        def hand(h, m, total):
            k = offset(h, m)
            total = total.astype(BF)
            if OFFSETS[0][m]:
                ret[j, h, m] = total
                r_copy(h, m, k).start()
            else:
                here = (mine == h) & jnp.logical_not(has_next)

                @pl.when(here)
                def _():
                    retin[2, 0] = total

                @pl.when(jnp.logical_not(here))
                def _():
                    ret[j, h, m] = total
                    r_copy(h, m, k).start()

        def give_back(h):
            @pl.when(initial)
            def _():
                for m in FAR_BLOCKS:
                    for d in (1, 3, 2):
                        p_copy(h, d, m).wait_recv()
                    total = pown[h, m]
                    for d in (1, 2, 3):
                        total = total + pin[h, d - 1, m].astype(F32)
                    hand(h, m, total)

            @pl.when(jnp.logical_not(initial))
            def _():
                for g in (1, 0):
                    ms = range(g * NB // 2, (g + 1) * NB // 2)
                    total = pown[h, ms.start : ms.stop]
                    for d in (1, 3, 2):
                        act_copy(h, d, g).wait_recv()
                        rows = slice(g * GROWS, (g + 1) * GROWS)
                        total = total + all_of(actin[j, h, d - 1, rows], (x + NX - d) % NX)
                    for m in ms[::-1]:
                        hand(h, m, total[m - ms.start])

        for h in range(NH):
            give_back(h)
        pl.when(initial)(w_wait)
        pl.when(initial)(start_spread)
        pl.when(j == 1)(lambda: finish(0))

        @pl.when(jnp.logical_not(has_next))
        def _():
            others = retin.at[2, pl.ds(1, NZ - 1)]
            remote(others, others, r_ss.at[j, 0], r_rs.at[2], zpeer(4)).wait_recv()
            branch = jnp.dot(wcomb[b], retin[2].reshape(ROWS, FS), preferred_element_type=F32)
            stash(j, (xcur[j].astype(F32) + branch).astype(BF))

        return carry

    lax.fori_loop(0, 2, job, 0)
    pl.when(jnp.logical_not(outer))(lambda: stash_back(1))

    finish(1)
    jf = jnp.where(low, 0, 1)
    out_ref[0:TOK, :] = out_f32[jf].astype(BF)
    out_ref[TOK : 2 * TOK, :] = out_f32[1 - jf].astype(BF)

    for j in range(2):
        remote(st_out.at[j, few], st_in.at[j, few], st_ss.at[j], st_rs.at[j], sib).wait_send()
    remote(tall.at[few], tall.at[few], t_ss.at[0], t_rs.at[0], sib).wait_send()
    for b in range(2):
        w_copy(b).wait_send()
    for cp in sibling_gate_up():
        cp.wait_send()
    all_spread().wait_send()

    @pl.when(outer)
    def _():
        remote(tokx.at[few], xin.at[few], tok_ss.at[0], tok_rs.at[0], sib).wait_send()
        for q in range(NX):
            sibling_down(q).wait_send()
        for h in range(NH):
            for d in (1, 2, 3):
                here = pout.at[h, d - 1]
                remote(here, here, p_ss.at[h, d - 1], p_rs.at[h, d - 1, 0], xpeer(d)).wait_send()

    def drain(j):
        b = jnp.where(low, j, 1 - j)
        to = s + 1 - 2 * b
        has_next = (to >= 0) & (to < NS)

        sent = dout.at[j, pl.ds(1, NZ - 1)]
        remote(sent, sent, d_ss.at[j], d_rs.at[j, 0, 0], zpeer(4)).wait_send()

        @pl.when(has_next)
        def _():
            remote(xcur.at[j], xcur.at[j], x_ss.at[j], x_rs.at[j], zpeer(4)).wait_send()

        @pl.when(jnp.logical_not(outer & (j == 0)))
        def _():
            remote(xcur.at[j], xcur.at[j], xb_ss.at[j], xb_rs.at[j], zpeer(4)).wait_send()

        for h in range(NH):
            for d in (1, 2, 3):
                here = rin.at[j, h, 0]
                remote(here, here, ag_ss.at[j, h, d - 1], ag_rs.at[j, h, d - 1], xpeer(d)).wait_send()

            here, fewer = ret.at[j, h], ret.at[j, h, pl.ds(0, NB - 1)]
            whole = (mine != h) | has_next
            pl.when(whole)(lambda: remote(here, here, r_ss.at[j, h], r_rs.at[j], zpeer(4)).wait_send())
            pl.when(jnp.logical_not(whole))(lambda: remote(fewer, fewer, r_ss.at[j, h], r_rs.at[j], zpeer(4)).wait_send())

            @pl.when(jnp.logical_not(outer & (j == 0)))
            def _():
                here = actin.at[j, h]
                remote(here, here, a_ss.at[j, h], a_rs.at[j, h, 0, 0], sib).wait_send()

            remote(guout.at[j, h], guin.at[j, h], gu_ss.at[j, h], gu_rs.at[j, h], sib).wait_send()

    loop(2, drain)


def split(both_ref, outf_ref, outr_ref):
    outf_ref[0] = both_ref[0:TOK, :]
    outr_ref[0] = both_ref[TOK : 2 * TOK, :]


def run(tokens_fwd, tokens_rev, routes_fwd, routes_rev, weights_fwd, weights_rev, norm_gain, gate_proj, up_proj, down_proj):
    vmem = pl.BlockSpec(memory_space=pltpu.VMEM)
    hbm = pl.BlockSpec(memory_space=pl.ANY)
    dma = pltpu.SemaphoreType.DMA
    out = jax.ShapeDtypeStruct((2 * TOK, D), BF)
    wide = 2 * NC * PIECE
    small = [a[0].T for a in (routes_fwd, routes_rev, weights_fwd, weights_rev)]
    both = pl.pallas_call(
        kernel,
        name="moe_pipeline",
        out_shape=out,
        in_specs=[hbm] * 10,
        out_specs=vmem,
        scratch_shapes=[
            pltpu.VMEM((TOK, D), BF),
            pltpu.VMEM((TOPK, TOK), jnp.int32),
            pltpu.VMEM((TOPK, TOK), jnp.int32),
            pltpu.VMEM((TOPK, TOK), BF),
            pltpu.VMEM((TOPK, TOK), BF),
            pltpu.VMEM((1, D), BF),
            pltpu.VMEM((2, TOK, D), F32),
            dma((6,)),
            pltpu.VMEM((NC, HALF, PIECE), BF),
            pltpu.VMEM((NC, HALF, PIECE), BF),
            pltpu.VMEM((NX, NC * PIECE, FS), BF),
            pltpu.VMEM((NP, PIECE, FS), BF),
            pltpu.VMEM((NP, 2 * TOK, 128), F32),
            pltpu.VMEM((NP, 2 * TOK, HALFWAY), BF),
            pltpu.VMEM((NP, 2 * TOK, HALFWAY), BF),
            pltpu.VMEM((NP, TOK, FS), F32),
            pltpu.VMEM((2, ROWS, 128), BF),
            pltpu.VMEM((2, PT, ROWS), BF),
            pltpu.VMEM((2, PT, ROWS), BF),
            pltpu.VMEM((2, NH, NX, NB, BLK, FS), BF),
            pltpu.VMEM((HROWS, wide), F32),
            pltpu.VMEM((HROWS, 128), F32),
            pltpu.VMEM((2, NH, HROWS, wide + 128), BF),
            pltpu.VMEM((2, NH, HROWS, wide + 128), BF),
            pltpu.VMEM((2, NH, HROWS, NC * PIECE), BF),
            pltpu.VMEM((2, NH, NX - 1, HROWS, NC * PIECE), BF),
            pltpu.VMEM((NH, NX - 1, NB, BLK, FS), BF),
            pltpu.VMEM((NH, NB, BLK, FS), F32),
            pltpu.VMEM((NH, NX - 1, NB, BLK, FS), BF),
            pltpu.VMEM((2, NH, NB, BLK, FS), BF),
            pltpu.VMEM((3, NZ, BLK, FS), BF),
            pltpu.VMEM((2, NZ, BLK, FS), BF),
            pltpu.VMEM((2, PT, FS), BF),
            pltpu.VMEM((2, PT, FS), BF),
            pltpu.VMEM((2, PT, FS), BF),
            pltpu.VMEM((2, NP, 2 * TOK, HALFWAY), BF),
            pltpu.VMEM((2, NP, 2 * TOK, HALFWAY), BF),
            dma((1,)), dma((1,)), dma((1,)), dma((1,)), dma((2,)), dma((2,)),
            dma((2 + NX,)), dma((2 + NX,)), dma((2 + NX,)),
            dma((1,)), dma((1,)), dma((1,)), dma((2, NH)), dma((2, NH, NX - 1, 2)),
            dma((2,)), dma((2, NH, NB)),
            dma((2, NH, NX - 1)), dma((2, NH, NX - 1)), dma((2, NH)), dma((2, NH)),
            dma((NH, NX - 1)), dma((NH, NX - 1, NB)), dma((2, NH)), dma((3,)),
            dma((2,)), dma((2,)), dma((2,)), dma((2,)), dma((2,)), dma((2,)),
        ],
        compiler_params=pltpu.CompilerParams(
            collective_id=0, has_side_effects=True, vmem_limit_bytes=56 * 2**20
        ),
    )(tokens_fwd, tokens_rev, *small, norm_gain, gate_proj, up_proj, down_proj)
    one = jax.ShapeDtypeStruct((1, TOK, D), BF)
    return pl.pallas_call(
        split, name="split", out_shape=(one, one), in_specs=[vmem], out_specs=(vmem, vmem)
    )(both)


def solution(mesh):
    placed = (
        P("expert", None),
        P("expert", None),
        P("section", "expert", None),
        P("section", "expert", None),
        P("section", "expert", None),
        P("section", "expert", None),
        P("section", None),
        P("section", None, "expert"),
        P("section", None, "expert"),
        P("section", "expert", None),
    )
    return jax.shard_map(
        run,
        mesh=mesh,
        in_specs=placed,
        out_specs=(P("section", "expert", None), P("section", "expert", None)),
        check_vma=False,
    )
```

```python
import functools

import jax
import jax.numpy as jnp
from jax import lax
from jax.experimental import pallas as pl
from jax.experimental.pallas import tpu as pltpu
from jax.sharding import PartitionSpec as P

MESH = pl.DeviceIdType.MESH
NS, NZ, NX, NC = 4, 8, 4, 2
NP = NX * NC
TOK = 8
LIVE = NZ
TOPK = 2
SLOT = 2
D = 7168
PIECE = 256
FS = D // NP
HALF = D // NC
ROWS = NZ * NP * SLOT
BLK = NP * SLOT
PT = NP * TOK
HALFWAY = 512
NH = 2
NB = NZ // NH
HROWS = ROWS // NH
GROUPS = (2, 4)
OFFSETS = ((0, 2, 6, 4), (1, 7, 3, 5))
NEAR_FIRST = (1, 7, 2, 6, 3, 5, 4)
FAR_BLOCKS = (3, 1, 2, 0)
BF, F32 = jnp.bfloat16, jnp.float32


def place(k):
    return OFFSETS[k % NH].index(-k % NZ)


def pack(value):
    return jnp.concatenate([value[:, 0:HALFWAY], value[:, FS - HALFWAY : FS]], axis=0).astype(BF)


def unpack(packed, ref, start):
    value = packed.astype(F32)
    ref[:, start : start + HALFWAY] = value[0:TOK]
    ref[:, start + FS - HALFWAY : start + FS] = value[TOK : 2 * TOK]


def nt_dot(a, b):
    return lax.dot_general(a, b, (((1,), (1,)), ((), ())), preferred_element_type=F32)


def kernel(
    tokf_hbm, tokr_hbm, rf_hbm, rr_hbm, wf_hbm, wr_hbm, gain_hbm, gate_hbm, up_hbm, down_hbm,
    out_ref,
    tok_ref, rf_ref, rr_ref, wf_ref, wr_ref, gain_ref, out_f32, in_s,
    wg, wu, wd, wall, tall, tokx, xin, plane32, sown, wcomb, wbefore, rin, acc, ssq, guout, guin, act, actin,
    pout, pown, pin, ret, retin, dout, xcur, xres, xback, st_out, st_in,
    t_ss, t_rs, tok_ss, tok_rs, s_ss, s_rs, wl_s, w_ss, w_rs, wa_l, wa_ss, wa_rs, a_ss, a_rs,
    d_ss, d_rs, ag_ss, ag_rs, gu_ss, gu_rs, p_ss, p_rs, r_ss, r_rs, x_ss, x_rs, xb_ss, xb_rs, st_ss, st_rs,
):
    s = lax.axis_index("section")
    i = lax.axis_index("expert")
    z, p = i // NP, i % NP
    x, c = p // NC, p % NC
    outer = (s == 0) | (s == NS - 1)
    inner = jnp.logical_not(outer)
    low = s < NS // 2

    def at(sec, zz, pp):
        return (sec, zz * NP + pp)

    def plane(r):
        return at(s, z, (p + r) % NP)

    def xpeer(d):
        return at(s, z, ((x + d) % NX) * NC + c)

    def zpeer(k):
        return at(s, (z + k) % NZ, p)

    sib = at(s, z, x * NC + 1 - c)
    q_far = (x + 2) % NX
    up_sec, down_sec = (s + 1) % NS, (s + NS - 1) % NS

    def remote(src, dst, ss, rs, dev):
        return pltpu.make_async_remote_copy(
            src_ref=src, dst_ref=dst, send_sem=ss, recv_sem=rs, device_id=dev, device_id_type=MESH
        )

    def loop(n, f):
        def step(n_, carry):
            f(n_)
            return carry

        lax.fori_loop(0, n, step, 0)

    bar = pltpu.get_barrier_semaphore()

    def greet(dev):
        pl.semaphore_signal(bar, inc=1, device_id=dev, device_id_type=MESH)

    loop(NP - 1, lambda r: greet(plane(r + 1)))
    loop(NZ - 1, lambda k: greet(zpeer(k + 1)))
    loop(NZ, lambda k: greet(at(up_sec, (z + k) % NZ, p)))
    loop(NZ, lambda k: greet(at(down_sec, (z + k) % NZ, p)))

    small = [
        pltpu.make_async_copy(src, dst, in_s.at[n])
        for n, (src, dst) in enumerate(
            ((rf_hbm, rf_ref), (rr_hbm, rr_ref), (wf_hbm, wf_ref), (wr_hbm, wr_ref), (gain_hbm, gain_ref))
        )
    ]
    for cp in small:
        cp.start()
    tokens = [pltpu.make_async_copy(src, tok_ref, in_s.at[5]) for src in (tokf_hbm, tokr_hbm)]
    pl.when(s == 0)(lambda: tokens[0].start())
    pl.when(s == NS - 1)(lambda: tokens[1].start())

    def half(core):
        return pl.ds(core * HALF, HALF)

    def slice_of(xx, core):
        return pl.ds(pl.multiple_of(core * HALF + xx * FS, 128), FS)

    def local_gate_up():
        return [
            pltpu.make_async_copy(gate_hbm.at[0, half(c), :], wg.at[c], wl_s.at[0]),
            pltpu.make_async_copy(up_hbm.at[0, half(c), :], wu.at[c], wl_s.at[1]),
        ]

    def sibling_gate_up():
        return [
            remote(gate_hbm.at[0, half(1 - c), :], wg.at[c], w_ss.at[0], w_rs.at[0], sib),
            remote(up_hbm.at[0, half(1 - c), :], wu.at[c], w_ss.at[1], w_rs.at[1], sib),
        ]

    def local_down(q):
        return pltpu.make_async_copy(
            down_hbm.at[0, :, slice_of(q, c)], wd.at[q, pl.ds(c * PIECE, PIECE), :], wl_s.at[2 + q]
        )

    def sibling_down(q):
        return remote(
            down_hbm.at[0, :, slice_of(q, 1 - c)], wd.at[q, pl.ds(c * PIECE, PIECE), :], w_ss.at[2 + q], w_rs.at[2 + q], sib
        )

    def local_spread():
        return pltpu.make_async_copy(down_hbm.at[0, :, slice_of(x, c)], wall.at[p], wa_l.at[0])

    def spread(q):
        return remote(
            down_hbm.at[0, :, slice_of(q // NC, q % NC)], wall.at[p], wa_ss.at[0], wa_rs.at[0], at(s, z, q)
        )

    def all_spread(count):
        some = wall.at[pl.ds(0, count)]
        return remote(some, some, wa_ss.at[0], wa_rs.at[0], sib)

    def start_spread():
        local_spread().start()
        for d in (1, 3):
            for o in range(NC):
                spread((x + d) % NX * NC + o).start()
        spread(x * NC + 1 - c).start()

        @pl.when(outer)
        def _():
            for o in range(NC):
                spread((x + 2) % NX * NC + o).start()

    def wait_spread():
        local_spread().wait()
        pl.when(outer)(lambda: all_spread(NP - 1).wait_recv())
        pl.when(inner)(lambda: all_spread(NP - 1 - NC).wait_recv())

    for cp in local_gate_up():
        cp.start()

    @pl.when(outer)
    def _():
        for q in range(NX):
            local_down(q).start()

    pl.when(inner)(lambda: local_down(q_far).start())

    for cp in small:
        cp.wait()
    ei = lax.broadcasted_iota(jnp.int32, (2 * LIVE, TOK), 0)
    eye = jnp.where(
        lax.broadcasted_iota(jnp.int32, (TOK, TOK), 0) == lax.broadcasted_iota(jnp.int32, (TOK, TOK), 1), 1.0, 0.0
    )
    for b, (routes, weights) in enumerate(((rf_ref, wf_ref), (rr_ref, wr_ref))):
        turned = jnp.zeros((2 * LIVE, TOK), F32)
        for n in range(TOPK):
            route, weight = routes[n : n + 1, :], weights[n : n + 1, :].astype(F32)
            turned += jnp.where(route == ei, 1.0, 0.0) + jnp.where(route == ei - LIVE, weight, 0.0)
        tall[p, b * TOK : (b + 1) * TOK, :] = jnp.zeros((TOK, 128), F32)
        tall[p, b * TOK : (b + 1) * TOK, 0 : 2 * LIVE] = nt_dot(eye, turned)

    @pl.when(outer)
    def _():
        tokens[0].wait()
        for q in range(NP):
            f = (q % NC) * NX + q // NC
            sl = slice(f * FS, (f + 1) * FS)
            tokx[q] = pack(tok_ref[:, sl].astype(F32))

    pl.semaphore_wait(bar, NP - 1 + NZ - 1 + 2 * NZ)

    def t_copy(r):
        return remote(tall.at[p], tall.at[p], t_ss.at[0], t_rs.at[0], plane(r + 1))

    few = pl.ds(0, NP - 1)

    def tok_copy(r):
        return remote(tokx.at[(p + r + 1) % NP], xin.at[p], tok_ss.at[0], tok_rs.at[0], plane(r + 1))

    loop(NP - 1, lambda r: t_copy(r).start())

    @pl.when(outer)
    def _():
        loop(NP - 1, lambda r: tok_copy(r).start())

    for cp in sibling_gate_up():
        cp.start()

    @pl.when(outer)
    def _():
        for q in range(NX):
            sibling_down(q).start()

    @pl.when(inner)
    def _():
        sibling_down(q_far).start()
        start_spread()


    @pl.when(outer)
    def _():
        xin[p] = tokx[p]

    remote(tall.at[few], tall.at[few], t_ss.at[0], t_rs.at[0], sib).wait_recv()

    row = lax.broadcasted_iota(jnp.int32, (ROWS, 128), 0)
    col = lax.broadcasted_iota(jnp.int32, (ROWS, 128), 1)
    pick = jnp.where(col == (z + row // BLK) % NZ, 1.0, 0.0)
    pick_w = jnp.where(col - NZ == (z + row // BLK) % NZ, 1.0, 0.0)
    ti = lax.broadcasted_iota(jnp.int32, (PT, PT), 0)
    tj = lax.broadcasted_iota(jnp.int32, (PT, PT), 1)
    before = jnp.where((ti // TOK == tj // TOK) & (tj < ti), 1.0, 0.0)
    srow = lax.broadcasted_iota(jnp.int32, (ROWS, PT), 0)
    scol = lax.broadcasted_iota(jnp.int32, (ROWS, PT), 1)
    trow = lax.broadcasted_iota(jnp.int32, (PT, ROWS), 0)
    tcol = lax.broadcasted_iota(jnp.int32, (PT, ROWS), 1)
    for b in range(2):
        t = tall[:, b * TOK : (b + 1) * TOK, :].reshape(PT, 128)
        rank = jnp.dot(before, t, preferred_element_type=F32)
        here = nt_dot(pick, t) * jnp.where(srow // SLOT % NP == scol // TOK, 1.0, 0.0)
        right = jnp.where(nt_dot(pick, rank) == (srow % SLOT).astype(F32), 1.0, 0.0)
        sown[b, :, 0:PT] = (here * right).astype(BF)
        sown[b, :, PT:128] = jnp.zeros((ROWS, 128 - PT), BF)
        here = nt_dot(t, pick_w) * jnp.where(tcol // SLOT % NP == trow // TOK, 1.0, 0.0)
        right = jnp.where(nt_dot(rank, pick) == (tcol % SLOT).astype(F32), 1.0, 0.0)
        wcomb[b] = (here * right).astype(BF)

    def w_copy(b):
        sec = up_sec if b == 0 else down_sec
        return remote(wcomb.at[b], wbefore.at[b], s_ss.at[b], s_rs.at[b], at(sec, z, p))

    for b in range(2):
        w_copy(b).start()

    @pl.when(outer)
    def _():
        remote(tokx.at[few], xin.at[few], tok_ss.at[0], tok_rs.at[0], sib).wait_recv()
        for q in range(NP):
            unpack(xin[q], plane32.at[q], 0)
        xcur[0] = plane32[...].reshape(PT, FS).astype(BF)

    mine = z % NH

    def st_copy(j, r):
        return remote(
            st_out.at[j, (p + r + 1) % NP], st_in.at[j, p], st_ss.at[j], st_rs.at[j], plane(r + 1)
        )

    def stash(j, value):
        value = value.astype(F32).reshape(NP, TOK, FS)
        for q in range(NP):
            st_out[j, q] = pack(value[q])
        st_in[j, p] = st_out[j, p]
        loop(NP - 1, lambda r: st_copy(j, r).start())

    def finish(j):
        remote(st_out.at[j, few], st_in.at[j, few], st_ss.at[j], st_rs.at[j], sib).wait_recv()
        for q in range(NP):
            f = (q % NC) * NX + q // NC
            unpack(st_in[j, q], out_f32.at[j], f * FS)

    def stash_back(j):
        remote(xback.at[j], xback.at[j], xb_ss.at[j], xb_rs.at[j], zpeer(4)).wait_recv()
        stash(j, xback[j])

    def w_wait():
        for b in range(2):
            w_copy(b).wait_recv()

    def job(j, carry):
        b = jnp.where(low, j, 1 - j)
        step = 1 - 2 * b
        initial = outer & (j == 0)
        to = s + step
        has_next = (to >= 0) & (to < NS)
        to = jnp.clip(to, 0, NS - 1)
        jn = jnp.where(to < NS // 2, b, 1 - b)
        came = jnp.clip(s - step, 0, NS - 1)
        jc = jnp.where(came < NS // 2, b, 1 - b)
        dest, slot = jnp.where(has_next, to, s), jnp.where(has_next, jn, 2)

        @pl.when(jnp.logical_not(initial))
        def _():
            pl.when(j == 0)(w_wait)
            remote(xres.at[j], xres.at[j], x_ss.at[j], x_rs.at[j], zpeer(4)).wait_recv()
            remote(retin.at[j], retin.at[j], r_ss.at[j, 0], r_rs.at[j], zpeer(4)).wait_recv()
            branch = jnp.dot(wbefore[b], retin[j].reshape(ROWS, FS), preferred_element_type=F32)
            xcur[j] = (xres[j].astype(F32) + branch).astype(BF)

        picked = jnp.dot(sown[b, :, 0:PT], xcur[j], preferred_element_type=F32).astype(BF)
        dout[j] = picked.reshape(NZ, BLK, FS)
        rin[j, mine, 0, place(0)] = picked[0:BLK]
        for k in NEAR_FIRST:
            remote(
                dout.at[j, k], rin.at[j, mine, 0, place(k)], d_ss.at[j], d_rs.at[j, mine, place(k)], zpeer(k)
            ).start()

        @pl.when(has_next)
        def _():
            remote(xcur.at[j], xres.at[jn], x_ss.at[j], x_rs.at[jn], at(to, z, p)).start()

        @pl.when(jnp.logical_not(initial))
        def _():
            remote(xcur.at[j], xback.at[jc], xb_ss.at[j], xb_rs.at[jc], at(came, z, p)).start()

        def offset(h, m):
            return jnp.where(mine == h, OFFSETS[0][m], OFFSETS[1][m])

        def d_wait(h, m):
            here = rin.at[j, h, 0, m]
            remote(here, here, d_ss.at[j], d_rs.at[j, h, m], zpeer(4)).wait_recv()

        def ag_copy(h, d, m):
            return remote(
                rin.at[j, h, 0, m], rin.at[j, h, d, m], ag_ss.at[j, h, d - 1], ag_rs.at[j, h, d - 1], xpeer(d)
            )

        def relay(h):
            for m in range(NB):
                if OFFSETS[0][m] == 0:

                    @pl.when(mine != h)
                    def _():
                        d_wait(h, m)
                else:
                    d_wait(h, m)
                for d in (2, 1, 3):
                    ag_copy(h, d, m).start()

        for h in range(NH):
            relay(h)

        pl.when(j == 1)(lambda: stash_back(0))

        @pl.when(j == 0)
        def _():
            for cp in local_gate_up():
                cp.wait()
            for cp in sibling_gate_up():
                cp.wait_recv()

        wide, hid = 2 * NC * PIECE, NC * PIECE

        def slice_product(hs, d):
            q = (x + NX - d) % NX
            rows = rin[j, hs.start : hs.stop, d].reshape(-1, FS).astype(F32)
            mine_rows = slice(hs.start * HROWS, hs.stop * HROWS)
            g = gain_ref[:, pl.ds(pl.multiple_of(c * HALF + q * FS, 128), FS)].astype(F32)
            ss = jnp.sum(rows * rows, axis=1, keepdims=True)
            u = (rows * g).astype(BF)
            at_row = pl.ds(pl.multiple_of(q * FS, 128), FS)
            for n, w in enumerate((wg, wu)):
                for o in range(NC):
                    sl = slice((n * NC + o) * PIECE, (n * NC + o + 1) * PIECE)
                    part = jnp.dot(u, w[o, at_row, :], preferred_element_type=F32)
                    acc[mine_rows, sl] = acc[mine_rows, sl] + part if d else part
            ss = jnp.broadcast_to(ss, (rows.shape[0], 128))
            ssq[mine_rows] = ssq[mine_rows] + ss if d else ss

        def p_copy(h, d, g):
            n = d - 1 - j
            return remote(
                pout.at[h, n, g], pin.at[h, n, g], p_ss.at[h, n], p_rs.at[h, n, g], xpeer(d)
            )

        def act_copy(h, d, g):
            rows = pl.ds(g * HROWS // GROUPS[h], HROWS // GROUPS[h])
            return remote(
                act.at[j, h, rows], actin.at[j, h, d - 1, rows], a_ss.at[j, h], a_rs.at[j, h, d - 1, g], xpeer(d)
            )

        def all_of(value, q):
            w = wall[pl.ds(q * NC, NC)].reshape(NC * PIECE, FS)
            return jnp.dot(value, w, preferred_element_type=F32).reshape(-1, BLK, FS)

        def gu_copy(h):
            return remote(guout.at[j, h], guin.at[j, h], gu_ss.at[j, h], gu_rs.at[j, h], sib)

        def products(h):
            for d in (1, 3, 2):
                remote(rin.at[j, h, 0], rin.at[j, h, d], ag_ss.at[j, h, d - 1], ag_rs.at[j, h, d - 1], sib).wait_recv()
                slice_product(range(h, h + 1), d)
            mine_rows = slice(h * HROWS, (h + 1) * HROWS)
            guout[j, h, :, 0:wide] = acc[mine_rows].astype(BF)
            ss = ssq[mine_rows]
            hi = ss.astype(BF)
            lo = (ss - hi.astype(F32)).astype(BF)
            lanes = lax.broadcasted_iota(jnp.int32, (HROWS, 128), 1)
            guout[j, h, :, wide:] = jnp.where(lanes == 0, hi, lo)
            gu_copy(h).start()

        def activation(h):
            gu_copy(h).wait_recv()
            mine_rows = slice(h * HROWS, (h + 1) * HROWS)
            ss = ssq[mine_rows, 0:1]
            ss = ss + guin[j, h, :, wide : wide + 1].astype(F32) + guin[j, h, :, wide + 1 : wide + 2].astype(F32)
            scale = lax.rsqrt(ss * (1.0 / D) + 1e-06)
            gate = (acc[mine_rows, 0:hid] + guin[j, h, :, 0:hid].astype(F32)) * scale
            upv = (acc[mine_rows, hid:wide] + guin[j, h, :, hid:wide].astype(F32)) * scale
            act[j, h] = (gate / (1.0 + jnp.exp(-gate)) * upv).astype(BF)

            @pl.when(initial)
            def _():
                if h == 0:
                    for q in range(NX):
                        local_down(q).wait()
                        sibling_down(q).wait_recv()
                for d in (2, 1, 3):
                    part = jnp.dot(act[j, h], wd[(x + d) % NX], preferred_element_type=F32)
                    pout[h, d - 1] = part.astype(BF).reshape(NB, BLK, FS)
                for g in FAR_BLOCKS:
                    for d in (2, 1, 3):
                        p_copy(h, d, g).start()
                pown[h] = jnp.dot(act[j, h], wd[x], preferred_element_type=F32).reshape(NB, BLK, FS)

            @pl.when(inner)
            def _():
                if h == 0:

                    @pl.when(j == 0)
                    def _():
                        local_down(q_far).wait()
                        sibling_down(q_far).wait_recv()

                part = jnp.dot(act[j, h], wd[q_far], preferred_element_type=F32)
                pout[h, 1 - j] = part.astype(BF).reshape(NB, BLK, FS)
                for g in FAR_BLOCKS:
                    p_copy(h, 2, g).start()

            @pl.when(jnp.logical_not(initial))
            def _():
                for g in range(GROUPS[h] - 1, -1, -1):
                    pl.when(outer)(lambda: act_copy(h, 2, g).start())
                    for d in (1, 3):
                        act_copy(h, d, g).start()

        def own_product(h):
            @pl.when(jnp.logical_not(initial))
            def _():
                if h == 0:
                    pl.when((j == 0) | outer)(wait_spread)
                pown[h] = all_of(act[j, h], x)

        slice_product(range(NH), 0)
        products(0)
        activation(0)
        products(1)
        own_product(0)
        activation(1)

        def r_copy(h, m, k):
            kk = (NZ - k) % NZ
            return remote(
                ret.at[j, h, m], retin.at[slot, kk], r_ss.at[j, h], r_rs.at[slot], at(dest, (z + k) % NZ, p)
            )

        def hand(h, m, total):
            k = offset(h, m)
            total = total.astype(BF)
            if OFFSETS[0][m]:
                ret[j, h, m] = total
                r_copy(h, m, k).start()
            else:
                here = (mine == h) & jnp.logical_not(has_next)

                @pl.when(here)
                def _():
                    retin[2, 0] = total

                @pl.when(jnp.logical_not(here))
                def _():
                    ret[j, h, m] = total
                    r_copy(h, m, k).start()

        def give_back(h):
            @pl.when(initial)
            def _():
                for m in FAR_BLOCKS:
                    for d in (1, 3, 2):
                        p_copy(h, d, m).wait_recv()
                    total = pown[h, m]
                    for d in (1, 2, 3):
                        total = total + pin[h, d - 1, m].astype(F32)
                    hand(h, m, total)

            @pl.when(jnp.logical_not(initial))
            def _():
                for g in range(GROUPS[h] - 1, -1, -1):
                    ms = range(g * NB // GROUPS[h], (g + 1) * NB // GROUPS[h])
                    total = pown[h, ms.start : ms.stop]
                    rows = slice(ms.start * BLK, ms.stop * BLK)

                    def add_chip(total, d):
                        act_copy(h, d, g).wait_recv()
                        return total + all_of(actin[j, h, d - 1, rows], (x + NX - d) % NX)

                    total = add_chip(add_chip(total, 1), 3)

                    @pl.when(outer)
                    def _():
                        whole = add_chip(total, 2)
                        for m in ms[::-1]:
                            hand(h, m, whole[m - ms.start])

                    @pl.when(inner)
                    def _():
                        for m in ms[::-1]:
                            p_copy(h, 2, m).wait_recv()
                            hand(h, m, total[m - ms.start] + pin[h, 1 - j, m].astype(F32))

        give_back(0)
        own_product(1)
        give_back(1)
        pl.when(initial)(w_wait)
        pl.when(initial)(start_spread)
        pl.when(j == 1)(lambda: finish(0))

        @pl.when(jnp.logical_not(has_next))
        def _():
            others = retin.at[2, pl.ds(1, NZ - 1)]
            remote(others, others, r_ss.at[j, 0], r_rs.at[2], zpeer(4)).wait_recv()
            branch = jnp.dot(wcomb[b], retin[2].reshape(ROWS, FS), preferred_element_type=F32)
            stash(j, (xcur[j].astype(F32) + branch).astype(BF))

        return carry

    lax.fori_loop(0, 2, job, 0)
    pl.when(jnp.logical_not(outer))(lambda: stash_back(1))

    finish(1)
    jf = jnp.where(low, 0, 1)
    out_ref[0:TOK, :] = out_f32[jf].astype(BF)
    out_ref[TOK : 2 * TOK, :] = out_f32[1 - jf].astype(BF)

    for j in range(2):
        remote(st_out.at[j, few], st_in.at[j, few], st_ss.at[j], st_rs.at[j], sib).wait_send()
    remote(tall.at[few], tall.at[few], t_ss.at[0], t_rs.at[0], sib).wait_send()
    for b in range(2):
        w_copy(b).wait_send()
    for cp in sibling_gate_up():
        cp.wait_send()
    pl.when(inner)(lambda: sibling_down(q_far).wait_send())
    pl.when(outer)(lambda: all_spread(NP - 1).wait_send())
    pl.when(inner)(lambda: all_spread(NP - 1 - NC).wait_send())

    @pl.when(outer)
    def _():
        remote(tokx.at[few], xin.at[few], tok_ss.at[0], tok_rs.at[0], sib).wait_send()
        for q in range(NX):
            sibling_down(q).wait_send()
        for h in range(NH):
            for d in (1, 2, 3):
                here = pout.at[h, d - 1]
                remote(here, here, p_ss.at[h, d - 1], p_rs.at[h, d - 1, 0], xpeer(d)).wait_send()

    def drain(j):
        b = jnp.where(low, j, 1 - j)
        to = s + 1 - 2 * b
        has_next = (to >= 0) & (to < NS)

        sent = dout.at[j, pl.ds(1, NZ - 1)]
        remote(sent, sent, d_ss.at[j], d_rs.at[j, 0, 0], zpeer(4)).wait_send()

        @pl.when(has_next)
        def _():
            remote(xcur.at[j], xcur.at[j], x_ss.at[j], x_rs.at[j], zpeer(4)).wait_send()

        @pl.when(jnp.logical_not(outer & (j == 0)))
        def _():
            remote(xcur.at[j], xcur.at[j], xb_ss.at[j], xb_rs.at[j], zpeer(4)).wait_send()

        for h in range(NH):
            for d in (1, 2, 3):
                here = rin.at[j, h, 0]
                remote(here, here, ag_ss.at[j, h, d - 1], ag_rs.at[j, h, d - 1], xpeer(d)).wait_send()

            here, fewer = ret.at[j, h], ret.at[j, h, pl.ds(0, NB - 1)]
            whole = (mine != h) | has_next
            pl.when(whole)(lambda: remote(here, here, r_ss.at[j, h], r_rs.at[j], zpeer(4)).wait_send())
            pl.when(jnp.logical_not(whole))(lambda: remote(fewer, fewer, r_ss.at[j, h], r_rs.at[j], zpeer(4)).wait_send())

            @pl.when(jnp.logical_not(outer & (j == 0)))
            def _():
                def act_sent(count):
                    here = actin.at[j, h, pl.ds(0, count)]
                    remote(here, here, a_ss.at[j, h], a_rs.at[j, h, 0, 0], sib).wait_send()

                pl.when(outer)(lambda: act_sent(NX - 1))

                @pl.when(inner)
                def _():
                    act_sent(2)
                    here = pout.at[h, 1 - j]
                    remote(here, here, p_ss.at[h, 1 - j], p_rs.at[h, 1 - j, 0], xpeer(2)).wait_send()

            remote(guout.at[j, h], guin.at[j, h], gu_ss.at[j, h], gu_rs.at[j, h], sib).wait_send()

    loop(2, drain)


def split(both_ref, outf_ref, outr_ref):
    outf_ref[0] = both_ref[0:TOK, :]
    outr_ref[0] = both_ref[TOK : 2 * TOK, :]


def run(tokens_fwd, tokens_rev, routes_fwd, routes_rev, weights_fwd, weights_rev, norm_gain, gate_proj, up_proj, down_proj):
    vmem = pl.BlockSpec(memory_space=pltpu.VMEM)
    hbm = pl.BlockSpec(memory_space=pl.ANY)
    dma = pltpu.SemaphoreType.DMA
    out = jax.ShapeDtypeStruct((2 * TOK, D), BF)
    wide = 2 * NC * PIECE
    small = [a[0].T for a in (routes_fwd, routes_rev, weights_fwd, weights_rev)]
    both = pl.pallas_call(
        kernel,
        name="moe_pipeline",
        out_shape=out,
        in_specs=[hbm] * 10,
        out_specs=vmem,
        scratch_shapes=[
            pltpu.VMEM((TOK, D), BF),
            pltpu.VMEM((TOPK, TOK), jnp.int32),
            pltpu.VMEM((TOPK, TOK), jnp.int32),
            pltpu.VMEM((TOPK, TOK), BF),
            pltpu.VMEM((TOPK, TOK), BF),
            pltpu.VMEM((1, D), BF),
            pltpu.VMEM((2, TOK, D), F32),
            dma((6,)),
            pltpu.VMEM((NC, HALF, PIECE), BF),
            pltpu.VMEM((NC, HALF, PIECE), BF),
            pltpu.VMEM((NX, NC * PIECE, FS), BF),
            pltpu.VMEM((NP, PIECE, FS), BF),
            pltpu.VMEM((NP, 2 * TOK, 128), F32),
            pltpu.VMEM((NP, 2 * TOK, HALFWAY), BF),
            pltpu.VMEM((NP, 2 * TOK, HALFWAY), BF),
            pltpu.VMEM((NP, TOK, FS), F32),
            pltpu.VMEM((2, ROWS, 128), BF),
            pltpu.VMEM((2, PT, ROWS), BF),
            pltpu.VMEM((2, PT, ROWS), BF),
            pltpu.VMEM((2, NH, NX, NB, BLK, FS), BF),
            pltpu.VMEM((ROWS, wide), F32),
            pltpu.VMEM((ROWS, 128), F32),
            pltpu.VMEM((2, NH, HROWS, wide + 128), BF),
            pltpu.VMEM((2, NH, HROWS, wide + 128), BF),
            pltpu.VMEM((2, NH, HROWS, NC * PIECE), BF),
            pltpu.VMEM((2, NH, NX - 1, HROWS, NC * PIECE), BF),
            pltpu.VMEM((NH, NX - 1, NB, BLK, FS), BF),
            pltpu.VMEM((NH, NB, BLK, FS), F32),
            pltpu.VMEM((NH, NX - 1, NB, BLK, FS), BF),
            pltpu.VMEM((2, NH, NB, BLK, FS), BF),
            pltpu.VMEM((3, NZ, BLK, FS), BF),
            pltpu.VMEM((2, NZ, BLK, FS), BF),
            pltpu.VMEM((2, PT, FS), BF),
            pltpu.VMEM((2, PT, FS), BF),
            pltpu.VMEM((2, PT, FS), BF),
            pltpu.VMEM((2, NP, 2 * TOK, HALFWAY), BF),
            pltpu.VMEM((2, NP, 2 * TOK, HALFWAY), BF),
            dma((1,)), dma((1,)), dma((1,)), dma((1,)), dma((2,)), dma((2,)),
            dma((2 + NX,)), dma((2 + NX,)), dma((2 + NX,)),
            dma((1,)), dma((1,)), dma((1,)), dma((2, NH)), dma((2, NH, NX - 1, max(GROUPS))),
            dma((2,)), dma((2, NH, NB)),
            dma((2, NH, NX - 1)), dma((2, NH, NX - 1)), dma((2, NH)), dma((2, NH)),
            dma((NH, NX - 1)), dma((NH, NX - 1, NB)), dma((2, NH)), dma((3,)),
            dma((2,)), dma((2,)), dma((2,)), dma((2,)), dma((2,)), dma((2,)),
        ],
        compiler_params=pltpu.CompilerParams(
            collective_id=0, has_side_effects=True, vmem_limit_bytes=56 * 2**20
        ),
    )(tokens_fwd, tokens_rev, *small, norm_gain, gate_proj, up_proj, down_proj)
    return both[None, 0:TOK], both[None, TOK : 2 * TOK]


def solution(mesh):
    placed = (
        P("expert", None),
        P("expert", None),
        P("section", "expert", None),
        P("section", "expert", None),
        P("section", "expert", None),
        P("section", "expert", None),
        P("section", None),
        P("section", None, "expert"),
        P("section", None, "expert"),
        P("section", "expert", None),
    )
    return jax.shard_map(
        run,
        mesh=mesh,
        in_specs=placed,
        out_specs=(P("section", "expert", None), P("section", "expert", None)),
        check_vma=False,
    )
```

```python
import functools

import jax
import jax.numpy as jnp
from jax import lax
from jax.experimental import pallas as pl
from jax.experimental.pallas import tpu as pltpu
from jax.sharding import PartitionSpec as P

MESH = pl.DeviceIdType.MESH
NS, NZ, NX, NC = 4, 8, 4, 2
NP = NX * NC
TOK = 8
LIVE = NZ
TOPK = 2
SLOT = 2
D = 7168
PIECE = 256
FS = D // NP
HALF = D // NC
ROWS = NZ * NP * SLOT
BLK = NP * SLOT
PT = NP * TOK
HALFWAY = 512
NH = 2
NB = NZ // NH
HROWS = ROWS // NH
GROUPS = (2, 4)
OFFSETS = ((0, 2, 6, 4), (1, 7, 3, 5))
NEAR_FIRST = (1, 7, 2, 6, 3, 5, 4)
FAR_BLOCKS = (3, 1, 2, 0)
BF, F32 = jnp.bfloat16, jnp.float32


def place(k):
    return OFFSETS[k % NH].index(-k % NZ)


def pack(value):
    return jnp.concatenate([value[:, 0:HALFWAY], value[:, FS - HALFWAY : FS]], axis=0).astype(BF)


def unpack(packed, ref, start):
    value = packed.astype(F32)
    ref[:, start : start + HALFWAY] = value[0:TOK]
    ref[:, start + FS - HALFWAY : start + FS] = value[TOK : 2 * TOK]


def nt_dot(a, b):
    return lax.dot_general(a, b, (((1,), (1,)), ((), ())), preferred_element_type=F32)


def kernel(
    tokf_ref, tokr_ref, rf_ref, rr_ref, wf_ref, wr_ref, gain_ref, gate_hbm, up_hbm, down_hbm,
    out_ref,
    out_f32,
    wg, wu, wd, wall, tall, tokx, xin, plane32, sown, wcomb, wbefore, rin, acc, ssq, guout, guin, act, actin,
    pout, pown, pin, ret, retin, dout, xcur, xres, xback, st_out, st_in,
    t_ss, t_rs, tok_ss, tok_rs, s_ss, s_rs, wl_s, w_ss, w_rs, wa_l, wa_ss, wa_rs, a_ss, a_rs,
    d_ss, d_rs, ag_ss, ag_rs, gu_ss, gu_rs, p_ss, p_rs, r_ss, r_rs, x_ss, x_rs, xb_ss, xb_rs, st_ss, st_rs,
):
    s = lax.axis_index("section")
    i = lax.axis_index("expert")
    z, p = i // NP, i % NP
    x, c = p // NC, p % NC
    outer = (s == 0) | (s == NS - 1)
    inner = jnp.logical_not(outer)
    low = s < NS // 2

    def at(sec, zz, pp):
        return (sec, zz * NP + pp)

    def plane(r):
        return at(s, z, (p + r) % NP)

    def xpeer(d):
        return at(s, z, ((x + d) % NX) * NC + c)

    def zpeer(k):
        return at(s, (z + k) % NZ, p)

    sib = at(s, z, x * NC + 1 - c)
    q_far = (x + 2) % NX
    up_sec, down_sec = (s + 1) % NS, (s + NS - 1) % NS

    def remote(src, dst, ss, rs, dev):
        return pltpu.make_async_remote_copy(
            src_ref=src, dst_ref=dst, send_sem=ss, recv_sem=rs, device_id=dev, device_id_type=MESH
        )

    def loop(n, f):
        def step(n_, carry):
            f(n_)
            return carry

        lax.fori_loop(0, n, step, 0)

    bar = pltpu.get_barrier_semaphore()

    def greet(dev):
        pl.semaphore_signal(bar, inc=1, device_id=dev, device_id_type=MESH)

    loop(NP - 1, lambda r: greet(plane(r + 1)))
    loop(NZ - 1, lambda k: greet(zpeer(k + 1)))
    loop(NZ, lambda k: greet(at(up_sec, (z + k) % NZ, p)))
    loop(NZ, lambda k: greet(at(down_sec, (z + k) % NZ, p)))

    def half(core):
        return pl.ds(core * HALF, HALF)

    def slice_of(xx, core):
        return pl.ds(pl.multiple_of(core * HALF + xx * FS, 128), FS)

    def local_gate_up():
        return [
            pltpu.make_async_copy(gate_hbm.at[0, half(c), :], wg.at[c], wl_s.at[0]),
            pltpu.make_async_copy(up_hbm.at[0, half(c), :], wu.at[c], wl_s.at[1]),
        ]

    def sibling_gate_up():
        return [
            remote(gate_hbm.at[0, half(1 - c), :], wg.at[c], w_ss.at[0], w_rs.at[0], sib),
            remote(up_hbm.at[0, half(1 - c), :], wu.at[c], w_ss.at[1], w_rs.at[1], sib),
        ]

    def local_down(q):
        return pltpu.make_async_copy(
            down_hbm.at[0, :, slice_of(q, c)], wd.at[q, pl.ds(c * PIECE, PIECE), :], wl_s.at[2 + q]
        )

    def sibling_down(q):
        return remote(
            down_hbm.at[0, :, slice_of(q, 1 - c)], wd.at[q, pl.ds(c * PIECE, PIECE), :], w_ss.at[2 + q], w_rs.at[2 + q], sib
        )

    def local_spread():
        return pltpu.make_async_copy(down_hbm.at[0, :, slice_of(x, c)], wall.at[p], wa_l.at[0])

    def spread(q):
        return remote(
            down_hbm.at[0, :, slice_of(q // NC, q % NC)], wall.at[p], wa_ss.at[0], wa_rs.at[0], at(s, z, q)
        )

    def all_spread(count):
        some = wall.at[pl.ds(0, count)]
        return remote(some, some, wa_ss.at[0], wa_rs.at[0], sib)

    def start_spread():
        local_spread().start()
        for d in (1, 3):
            for o in range(NC):
                spread((x + d) % NX * NC + o).start()
        spread(x * NC + 1 - c).start()

        @pl.when(outer)
        def _():
            for o in range(NC):
                spread((x + 2) % NX * NC + o).start()

    def wait_spread():
        local_spread().wait()
        pl.when(outer)(lambda: all_spread(NP - 1).wait_recv())
        pl.when(inner)(lambda: all_spread(NP - 1 - NC).wait_recv())

    for cp in local_gate_up():
        cp.start()

    @pl.when(outer)
    def _():
        for q in range(NX):
            local_down(q).start()

    pl.when(inner)(lambda: local_down(q_far).start())

    ei = lax.broadcasted_iota(jnp.int32, (2 * LIVE, TOK), 0)
    eye = jnp.where(
        lax.broadcasted_iota(jnp.int32, (TOK, TOK), 0) == lax.broadcasted_iota(jnp.int32, (TOK, TOK), 1), 1.0, 0.0
    )
    for b, (routes, weights) in enumerate(((rf_ref, wf_ref), (rr_ref, wr_ref))):
        turned = jnp.zeros((2 * LIVE, TOK), F32)
        for n in range(TOPK):
            route, weight = routes[n : n + 1, :], weights[n : n + 1, :].astype(F32)
            turned += jnp.where(route == ei, 1.0, 0.0) + jnp.where(route == ei - LIVE, weight, 0.0)
        tall[p, b * TOK : (b + 1) * TOK, :] = jnp.zeros((TOK, 128), F32)
        tall[p, b * TOK : (b + 1) * TOK, 0 : 2 * LIVE] = nt_dot(eye, turned)

    @pl.when(outer)
    def _():
        for q in range(NP):
            f = (q % NC) * NX + q // NC
            sl = slice(f * FS, (f + 1) * FS)
            tokx[q] = pack(jnp.where(s == 0, tokf_ref[:, sl].astype(F32), tokr_ref[:, sl].astype(F32)))

    pl.semaphore_wait(bar, NP - 1 + NZ - 1 + 2 * NZ)

    def t_copy(r):
        return remote(tall.at[p], tall.at[p], t_ss.at[0], t_rs.at[0], plane(r + 1))

    few = pl.ds(0, NP - 1)

    def tok_copy(r):
        return remote(tokx.at[(p + r + 1) % NP], xin.at[p], tok_ss.at[0], tok_rs.at[0], plane(r + 1))

    loop(NP - 1, lambda r: t_copy(r).start())

    @pl.when(outer)
    def _():
        loop(NP - 1, lambda r: tok_copy(r).start())

    for cp in sibling_gate_up():
        cp.start()

    @pl.when(outer)
    def _():
        for q in range(NX):
            sibling_down(q).start()

    @pl.when(inner)
    def _():
        sibling_down(q_far).start()
        start_spread()


    @pl.when(outer)
    def _():
        xin[p] = tokx[p]

    remote(tall.at[few], tall.at[few], t_ss.at[0], t_rs.at[0], sib).wait_recv()

    row = lax.broadcasted_iota(jnp.int32, (ROWS, 128), 0)
    col = lax.broadcasted_iota(jnp.int32, (ROWS, 128), 1)
    pick = jnp.where(col == (z + row // BLK) % NZ, 1.0, 0.0)
    pick_w = jnp.where(col - NZ == (z + row // BLK) % NZ, 1.0, 0.0)
    ti = lax.broadcasted_iota(jnp.int32, (PT, PT), 0)
    tj = lax.broadcasted_iota(jnp.int32, (PT, PT), 1)
    before = jnp.where((ti // TOK == tj // TOK) & (tj < ti), 1.0, 0.0)
    srow = lax.broadcasted_iota(jnp.int32, (ROWS, PT), 0)
    scol = lax.broadcasted_iota(jnp.int32, (ROWS, PT), 1)
    trow = lax.broadcasted_iota(jnp.int32, (PT, ROWS), 0)
    tcol = lax.broadcasted_iota(jnp.int32, (PT, ROWS), 1)
    for b in range(2):
        t = tall[:, b * TOK : (b + 1) * TOK, :].reshape(PT, 128)
        rank = jnp.dot(before, t, preferred_element_type=F32)
        here = nt_dot(pick, t) * jnp.where(srow // SLOT % NP == scol // TOK, 1.0, 0.0)
        right = jnp.where(nt_dot(pick, rank) == (srow % SLOT).astype(F32), 1.0, 0.0)
        sown[b, :, 0:PT] = (here * right).astype(BF)
        sown[b, :, PT:128] = jnp.zeros((ROWS, 128 - PT), BF)
        here = nt_dot(t, pick_w) * jnp.where(tcol // SLOT % NP == trow // TOK, 1.0, 0.0)
        right = jnp.where(nt_dot(rank, pick) == (tcol % SLOT).astype(F32), 1.0, 0.0)
        wcomb[b] = (here * right).astype(BF)

    def w_copy(b):
        sec = up_sec if b == 0 else down_sec
        return remote(wcomb.at[b], wbefore.at[b], s_ss.at[b], s_rs.at[b], at(sec, z, p))

    for b in range(2):
        w_copy(b).start()

    @pl.when(outer)
    def _():
        remote(tokx.at[few], xin.at[few], tok_ss.at[0], tok_rs.at[0], sib).wait_recv()
        for q in range(NP):
            unpack(xin[q], plane32.at[q], 0)
        xcur[0] = plane32[...].reshape(PT, FS).astype(BF)

    mine = z % NH

    def st_copy(j, r):
        return remote(
            st_out.at[j, (p + r + 1) % NP], st_in.at[j, p], st_ss.at[j], st_rs.at[j], plane(r + 1)
        )

    def stash(j, value):
        value = value.astype(F32).reshape(NP, TOK, FS)
        for q in range(NP):
            st_out[j, q] = pack(value[q])
        st_in[j, p] = st_out[j, p]
        loop(NP - 1, lambda r: st_copy(j, r).start())

    def finish(j):
        remote(st_out.at[j, few], st_in.at[j, few], st_ss.at[j], st_rs.at[j], sib).wait_recv()
        for q in range(NP):
            f = (q % NC) * NX + q // NC
            unpack(st_in[j, q], out_f32.at[j], f * FS)

    def stash_back(j):
        remote(xback.at[j], xback.at[j], xb_ss.at[j], xb_rs.at[j], zpeer(4)).wait_recv()
        stash(j, xback[j])

    def w_wait():
        for b in range(2):
            w_copy(b).wait_recv()

    def job(j, carry):
        b = jnp.where(low, j, 1 - j)
        step = 1 - 2 * b
        initial = outer & (j == 0)
        to = s + step
        has_next = (to >= 0) & (to < NS)
        to = jnp.clip(to, 0, NS - 1)
        jn = jnp.where(to < NS // 2, b, 1 - b)
        came = jnp.clip(s - step, 0, NS - 1)
        jc = jnp.where(came < NS // 2, b, 1 - b)
        dest, slot = jnp.where(has_next, to, s), jnp.where(has_next, jn, 2)

        @pl.when(jnp.logical_not(initial))
        def _():
            pl.when(j == 0)(w_wait)
            remote(xres.at[j], xres.at[j], x_ss.at[j], x_rs.at[j], zpeer(4)).wait_recv()
            remote(retin.at[j], retin.at[j], r_ss.at[j, 0], r_rs.at[j], zpeer(4)).wait_recv()
            branch = jnp.dot(wbefore[b], retin[j].reshape(ROWS, FS), preferred_element_type=F32)
            xcur[j] = (xres[j].astype(F32) + branch).astype(BF)

        picked = jnp.dot(sown[b, :, 0:PT], xcur[j], preferred_element_type=F32).astype(BF)
        dout[j] = picked.reshape(NZ, BLK, FS)
        rin[j, mine, 0, place(0)] = picked[0:BLK]
        for k in NEAR_FIRST:
            remote(
                dout.at[j, k], rin.at[j, mine, 0, place(k)], d_ss.at[j], d_rs.at[j, mine, place(k)], zpeer(k)
            ).start()

        @pl.when(has_next)
        def _():
            remote(xcur.at[j], xres.at[jn], x_ss.at[j], x_rs.at[jn], at(to, z, p)).start()

        @pl.when(jnp.logical_not(initial))
        def _():
            remote(xcur.at[j], xback.at[jc], xb_ss.at[j], xb_rs.at[jc], at(came, z, p)).start()

        def offset(h, m):
            return jnp.where(mine == h, OFFSETS[0][m], OFFSETS[1][m])

        def d_wait(h, m):
            here = rin.at[j, h, 0, m]
            remote(here, here, d_ss.at[j], d_rs.at[j, h, m], zpeer(4)).wait_recv()

        def ag_copy(h, d, m):
            return remote(
                rin.at[j, h, 0, m], rin.at[j, h, d, m], ag_ss.at[j, h, d - 1], ag_rs.at[j, h, d - 1], xpeer(d)
            )

        def relay(h):
            for m in range(NB):
                if OFFSETS[0][m] == 0:

                    @pl.when(mine != h)
                    def _():
                        d_wait(h, m)
                else:
                    d_wait(h, m)
                for d in (2, 1, 3):
                    ag_copy(h, d, m).start()

        for h in range(NH):
            relay(h)

        pl.when(j == 1)(lambda: stash_back(0))

        @pl.when(j == 0)
        def _():
            for cp in local_gate_up():
                cp.wait()
            for cp in sibling_gate_up():
                cp.wait_recv()

        wide, hid = 2 * NC * PIECE, NC * PIECE

        def slice_product(hs, d):
            q = (x + NX - d) % NX
            rows = rin[j, hs.start : hs.stop, d].reshape(-1, FS).astype(F32)
            mine_rows = slice(hs.start * HROWS, hs.stop * HROWS)
            g = gain_ref[:, pl.ds(pl.multiple_of(c * HALF + q * FS, 128), FS)].astype(F32)
            ss = jnp.sum(rows * rows, axis=1, keepdims=True)
            u = (rows * g).astype(BF)
            at_row = pl.ds(pl.multiple_of(q * FS, 128), FS)
            for n, w in enumerate((wg, wu)):
                for o in range(NC):
                    sl = slice((n * NC + o) * PIECE, (n * NC + o + 1) * PIECE)
                    part = jnp.dot(u, w[o, at_row, :], preferred_element_type=F32)
                    acc[mine_rows, sl] = acc[mine_rows, sl] + part if d else part
            ss = jnp.broadcast_to(ss, (rows.shape[0], 128))
            ssq[mine_rows] = ssq[mine_rows] + ss if d else ss

        def p_copy(h, d, g):
            n = d - 1 - j
            return remote(
                pout.at[h, n, g], pin.at[h, n, g], p_ss.at[h, n], p_rs.at[h, n, g], xpeer(d)
            )

        def act_copy(h, d, g):
            rows = pl.ds(g * HROWS // GROUPS[h], HROWS // GROUPS[h])
            return remote(
                act.at[j, h, rows], actin.at[j, h, d - 1, rows], a_ss.at[j, h], a_rs.at[j, h, d - 1, g], xpeer(d)
            )

        def all_of(value, q):
            w = wall[pl.ds(q * NC, NC)].reshape(NC * PIECE, FS)
            return jnp.dot(value, w, preferred_element_type=F32).reshape(-1, BLK, FS)

        def gu_copy(h):
            return remote(guout.at[j, h], guin.at[j, h], gu_ss.at[j, h], gu_rs.at[j, h], sib)

        def products(h):
            for d in (1, 3, 2):
                remote(rin.at[j, h, 0], rin.at[j, h, d], ag_ss.at[j, h, d - 1], ag_rs.at[j, h, d - 1], sib).wait_recv()
                slice_product(range(h, h + 1), d)
            mine_rows = slice(h * HROWS, (h + 1) * HROWS)
            guout[j, h, :, 0:wide] = acc[mine_rows].astype(BF)
            ss = ssq[mine_rows]
            hi = ss.astype(BF)
            lo = (ss - hi.astype(F32)).astype(BF)
            lanes = lax.broadcasted_iota(jnp.int32, (HROWS, 128), 1)
            guout[j, h, :, wide:] = jnp.where(lanes == 0, hi, lo)
            gu_copy(h).start()

        def activation(h):
            gu_copy(h).wait_recv()
            mine_rows = slice(h * HROWS, (h + 1) * HROWS)
            ss = ssq[mine_rows, 0:1]
            ss = ss + guin[j, h, :, wide : wide + 1].astype(F32) + guin[j, h, :, wide + 1 : wide + 2].astype(F32)
            scale = lax.rsqrt(ss * (1.0 / D) + 1e-06)
            gate = (acc[mine_rows, 0:hid] + guin[j, h, :, 0:hid].astype(F32)) * scale
            upv = (acc[mine_rows, hid:wide] + guin[j, h, :, hid:wide].astype(F32)) * scale
            act[j, h] = (gate / (1.0 + jnp.exp(-gate)) * upv).astype(BF)

            @pl.when(initial)
            def _():
                if h == 0:
                    for q in range(NX):
                        local_down(q).wait()
                        sibling_down(q).wait_recv()
                for d in (2, 1, 3):
                    part = jnp.dot(act[j, h], wd[(x + d) % NX], preferred_element_type=F32)
                    pout[h, d - 1] = part.astype(BF).reshape(NB, BLK, FS)
                for g in FAR_BLOCKS:
                    for d in (2, 1, 3):
                        p_copy(h, d, g).start()
                pown[h] = jnp.dot(act[j, h], wd[x], preferred_element_type=F32).reshape(NB, BLK, FS)

            @pl.when(inner)
            def _():
                if h == 0:

                    @pl.when(j == 0)
                    def _():
                        local_down(q_far).wait()
                        sibling_down(q_far).wait_recv()

                part = jnp.dot(act[j, h], wd[q_far], preferred_element_type=F32)
                pout[h, 1 - j] = part.astype(BF).reshape(NB, BLK, FS)
                for g in FAR_BLOCKS:
                    p_copy(h, 2, g).start()

            @pl.when(jnp.logical_not(initial))
            def _():
                for g in range(GROUPS[h] - 1, -1, -1):
                    pl.when(outer)(lambda: act_copy(h, 2, g).start())
                    for d in (1, 3):
                        act_copy(h, d, g).start()

        def own_product(h):
            @pl.when(jnp.logical_not(initial))
            def _():
                if h == 0:
                    pl.when((j == 0) | outer)(wait_spread)
                pown[h] = all_of(act[j, h], x)

        slice_product(range(NH), 0)
        products(0)
        activation(0)
        products(1)
        own_product(0)
        activation(1)

        def r_copy(h, m, k):
            kk = (NZ - k) % NZ
            return remote(
                ret.at[j, h, m], retin.at[slot, kk], r_ss.at[j, h], r_rs.at[slot], at(dest, (z + k) % NZ, p)
            )

        def hand(h, m, total):
            k = offset(h, m)
            total = total.astype(BF)
            if OFFSETS[0][m]:
                ret[j, h, m] = total
                r_copy(h, m, k).start()
            else:
                here = (mine == h) & jnp.logical_not(has_next)

                @pl.when(here)
                def _():
                    retin[2, 0] = total

                @pl.when(jnp.logical_not(here))
                def _():
                    ret[j, h, m] = total
                    r_copy(h, m, k).start()

        def give_back(h):
            @pl.when(initial)
            def _():
                for m in FAR_BLOCKS:
                    for d in (1, 3, 2):
                        p_copy(h, d, m).wait_recv()
                    total = pown[h, m]
                    for d in (1, 2, 3):
                        total = total + pin[h, d - 1, m].astype(F32)
                    hand(h, m, total)

            @pl.when(jnp.logical_not(initial))
            def _():
                for g in range(GROUPS[h] - 1, -1, -1):
                    ms = range(g * NB // GROUPS[h], (g + 1) * NB // GROUPS[h])
                    total = pown[h, ms.start : ms.stop]
                    rows = slice(ms.start * BLK, ms.stop * BLK)

                    def add_chip(total, d):
                        act_copy(h, d, g).wait_recv()
                        return total + all_of(actin[j, h, d - 1, rows], (x + NX - d) % NX)

                    total = add_chip(add_chip(total, 1), 3)

                    @pl.when(outer)
                    def _():
                        whole = add_chip(total, 2)
                        for m in ms[::-1]:
                            hand(h, m, whole[m - ms.start])

                    @pl.when(inner)
                    def _():
                        for m in ms[::-1]:
                            p_copy(h, 2, m).wait_recv()
                            hand(h, m, total[m - ms.start] + pin[h, 1 - j, m].astype(F32))

        give_back(0)
        own_product(1)
        give_back(1)
        pl.when(initial)(w_wait)
        pl.when(initial)(start_spread)
        pl.when(j == 1)(lambda: finish(0))

        @pl.when(jnp.logical_not(has_next))
        def _():
            others = retin.at[2, pl.ds(1, NZ - 1)]
            remote(others, others, r_ss.at[j, 0], r_rs.at[2], zpeer(4)).wait_recv()
            branch = jnp.dot(wcomb[b], retin[2].reshape(ROWS, FS), preferred_element_type=F32)
            stash(j, (xcur[j].astype(F32) + branch).astype(BF))

        return carry

    lax.fori_loop(0, 2, job, 0)
    pl.when(jnp.logical_not(outer))(lambda: stash_back(1))

    finish(1)
    jf = jnp.where(low, 0, 1)
    out_ref[...] = jnp.concatenate([out_f32[jf], out_f32[1 - jf]], axis=0).astype(BF)

    for j in range(2):
        remote(st_out.at[j, few], st_in.at[j, few], st_ss.at[j], st_rs.at[j], sib).wait_send()
    remote(tall.at[few], tall.at[few], t_ss.at[0], t_rs.at[0], sib).wait_send()
    for b in range(2):
        w_copy(b).wait_send()
    for cp in sibling_gate_up():
        cp.wait_send()
    pl.when(inner)(lambda: sibling_down(q_far).wait_send())
    pl.when(outer)(lambda: all_spread(NP - 1).wait_send())
    pl.when(inner)(lambda: all_spread(NP - 1 - NC).wait_send())

    @pl.when(outer)
    def _():
        remote(tokx.at[few], xin.at[few], tok_ss.at[0], tok_rs.at[0], sib).wait_send()
        for q in range(NX):
            sibling_down(q).wait_send()
        for h in range(NH):
            for d in (1, 2, 3):
                here = pout.at[h, d - 1]
                remote(here, here, p_ss.at[h, d - 1], p_rs.at[h, d - 1, 0], xpeer(d)).wait_send()

    def drain(j):
        b = jnp.where(low, j, 1 - j)
        to = s + 1 - 2 * b
        has_next = (to >= 0) & (to < NS)

        sent = dout.at[j, pl.ds(1, NZ - 1)]
        remote(sent, sent, d_ss.at[j], d_rs.at[j, 0, 0], zpeer(4)).wait_send()

        @pl.when(has_next)
        def _():
            remote(xcur.at[j], xcur.at[j], x_ss.at[j], x_rs.at[j], zpeer(4)).wait_send()

        @pl.when(jnp.logical_not(outer & (j == 0)))
        def _():
            remote(xcur.at[j], xcur.at[j], xb_ss.at[j], xb_rs.at[j], zpeer(4)).wait_send()

        for h in range(NH):
            for d in (1, 2, 3):
                here = rin.at[j, h, 0]
                remote(here, here, ag_ss.at[j, h, d - 1], ag_rs.at[j, h, d - 1], xpeer(d)).wait_send()

            here, fewer = ret.at[j, h], ret.at[j, h, pl.ds(0, NB - 1)]
            whole = (mine != h) | has_next
            pl.when(whole)(lambda: remote(here, here, r_ss.at[j, h], r_rs.at[j], zpeer(4)).wait_send())
            pl.when(jnp.logical_not(whole))(lambda: remote(fewer, fewer, r_ss.at[j, h], r_rs.at[j], zpeer(4)).wait_send())

            @pl.when(jnp.logical_not(outer & (j == 0)))
            def _():
                def act_sent(count):
                    here = actin.at[j, h, pl.ds(0, count)]
                    remote(here, here, a_ss.at[j, h], a_rs.at[j, h, 0, 0], sib).wait_send()

                pl.when(outer)(lambda: act_sent(NX - 1))

                @pl.when(inner)
                def _():
                    act_sent(2)
                    here = pout.at[h, 1 - j]
                    remote(here, here, p_ss.at[h, 1 - j], p_rs.at[h, 1 - j, 0], xpeer(2)).wait_send()

            remote(guout.at[j, h], guin.at[j, h], gu_ss.at[j, h], gu_rs.at[j, h], sib).wait_send()

    loop(2, drain)


def split(both_ref, outf_ref, outr_ref):
    outf_ref[0] = both_ref[0:TOK, :]
    outr_ref[0] = both_ref[TOK : 2 * TOK, :]


def run(tokens_fwd, tokens_rev, routes_fwd, routes_rev, weights_fwd, weights_rev, norm_gain, gate_proj, up_proj, down_proj):
    vmem = pl.BlockSpec(memory_space=pltpu.VMEM)
    hbm = pl.BlockSpec(memory_space=pl.ANY)
    dma = pltpu.SemaphoreType.DMA
    out = jax.ShapeDtypeStruct((2 * TOK, D), BF)
    wide = 2 * NC * PIECE
    small = [a[0].T for a in (routes_fwd, routes_rev, weights_fwd, weights_rev)]
    both = pl.pallas_call(
        kernel,
        name="moe_pipeline",
        out_shape=out,
        in_specs=[vmem] * 7 + [hbm] * 3,
        out_specs=vmem,
        scratch_shapes=[
            pltpu.VMEM((2, TOK, D), F32),
            pltpu.VMEM((NC, HALF, PIECE), BF),
            pltpu.VMEM((NC, HALF, PIECE), BF),
            pltpu.VMEM((NX, NC * PIECE, FS), BF),
            pltpu.VMEM((NP, PIECE, FS), BF),
            pltpu.VMEM((NP, 2 * TOK, 128), F32),
            pltpu.VMEM((NP, 2 * TOK, HALFWAY), BF),
            pltpu.VMEM((NP, 2 * TOK, HALFWAY), BF),
            pltpu.VMEM((NP, TOK, FS), F32),
            pltpu.VMEM((2, ROWS, 128), BF),
            pltpu.VMEM((2, PT, ROWS), BF),
            pltpu.VMEM((2, PT, ROWS), BF),
            pltpu.VMEM((2, NH, NX, NB, BLK, FS), BF),
            pltpu.VMEM((ROWS, wide), F32),
            pltpu.VMEM((ROWS, 128), F32),
            pltpu.VMEM((2, NH, HROWS, wide + 128), BF),
            pltpu.VMEM((2, NH, HROWS, wide + 128), BF),
            pltpu.VMEM((2, NH, HROWS, NC * PIECE), BF),
            pltpu.VMEM((2, NH, NX - 1, HROWS, NC * PIECE), BF),
            pltpu.VMEM((NH, NX - 1, NB, BLK, FS), BF),
            pltpu.VMEM((NH, NB, BLK, FS), F32),
            pltpu.VMEM((NH, NX - 1, NB, BLK, FS), BF),
            pltpu.VMEM((2, NH, NB, BLK, FS), BF),
            pltpu.VMEM((3, NZ, BLK, FS), BF),
            pltpu.VMEM((2, NZ, BLK, FS), BF),
            pltpu.VMEM((2, PT, FS), BF),
            pltpu.VMEM((2, PT, FS), BF),
            pltpu.VMEM((2, PT, FS), BF),
            pltpu.VMEM((2, NP, 2 * TOK, HALFWAY), BF),
            pltpu.VMEM((2, NP, 2 * TOK, HALFWAY), BF),
            dma((1,)), dma((1,)), dma((1,)), dma((1,)), dma((2,)), dma((2,)),
            dma((2 + NX,)), dma((2 + NX,)), dma((2 + NX,)),
            dma((1,)), dma((1,)), dma((1,)), dma((2, NH)), dma((2, NH, NX - 1, max(GROUPS))),
            dma((2,)), dma((2, NH, NB)),
            dma((2, NH, NX - 1)), dma((2, NH, NX - 1)), dma((2, NH)), dma((2, NH)),
            dma((NH, NX - 1)), dma((NH, NX - 1, NB)), dma((2, NH)), dma((3,)),
            dma((2,)), dma((2,)), dma((2,)), dma((2,)), dma((2,)), dma((2,)),
        ],
        compiler_params=pltpu.CompilerParams(
            collective_id=0, has_side_effects=True, vmem_limit_bytes=56 * 2**20
        ),
    )(tokens_fwd, tokens_rev, *small, norm_gain, gate_proj, up_proj, down_proj)
    return both[None, 0:TOK], both[None, TOK : 2 * TOK]


def solution(mesh):
    placed = (
        P("expert", None),
        P("expert", None),
        P("section", "expert", None),
        P("section", "expert", None),
        P("section", "expert", None),
        P("section", "expert", None),
        P("section", None),
        P("section", None, "expert"),
        P("section", None, "expert"),
        P("section", "expert", None),
    )
    return jax.shard_map(
        run,
        mesh=mesh,
        in_specs=placed,
        out_specs=(P("section", "expert", None), P("section", "expert", None)),
        check_vma=False,
    )
```
